128 devices in a mesh: bx: 8 (over x, z_lo), by: 16 (over z_hi, y, core).
Axes of the slice: x: 4, y: 4, z: 4 (z_hi: 2, z_lo: 2; z = z_hi * 2 + z_lo), core: 2. Of those that a mesh axis runs over, the one named last changes fastest.
Arguments:
- flow_field: float32 [4, 256, 384, 256], P(None, 'bx', 'by'), may hold values from -6 to 6
- patch_corners: int32 [3, 8, 512], P(None, 'bx', 'by'), may hold values from 0 to 240, as said below
- patch_learner: int32 [8, 512, 1], P('bx', 'by'), may hold values from 0 to 15; in each aligned block of 32 rows (0 to 31, 32 to 63, ..., all dimensions but the last counted through in order) at most 4 rows name the same one
- drag_target: bfloat16 [3, 8, 512], P(None, 'bx', 'by'), may hold values from -6 to 6
- embed_weight: float32 [256, 512], replicated, may hold values from -0.375 to 0.375
- mixer_weight: float32 [512, 512], replicated, may hold values from -0.25 to 0.25
- head_weight: float32 [3, 512], replicated, may hold values from -0.25 to 0.25
Outputs:
- advanced_flow: float32 [4, 256, 384, 256], P(None, 'bx', 'by')
- slot_drag: float32 [3, 8, 1024], P(None, 'bx', 'by')
- update_embed: float32 [256, 512], replicated
- update_mixer: float32 [512, 512], replicated
- update_head: float32 [3, 512], replicated
The draws below stay inside these ranges and needn't reach their ends.
Inputs may be any that keep to these rules, and one draw needn't show every extreme that they name: `patch_corners`: each patch lies inside its brick: the first two entries are at most 16 and 8, the third at most 240. `patch_learner`: the patches of one brick name any one learner at most 4 times, and every draw has a brick that names some learner exactly 4 times.
All inputs are finite; a program needn't handle non-finite values.
Results may differ from the reference program's by a relative error of at most 0.0053.
Values may be sent and summed in bfloat16 or wider, within the bound.
A program may use at most 128 MiB of HBM per device.

```python
import math
import jax
import jax.numpy as jnp
import numpy as np
from jax import lax

CX = 32
CY = 24
CZ = 256
CHAN = 4
PATCH = 16
CUBE = 4
HID = 512
PB = 32
CAP = 4
BRICKS_X = 8
BRICKS_Y = 16
NX = 256
NY = 384
FEAT = 256


def draw_patch_corners(key, part):
    key = jax.random.fold_in(key, 7)
    key_x, key_y, key_z = jax.random.split(key, 3)
    shape = (1, BRICKS_X, BRICKS_Y * PB)
    along_x = jax.random.randint(key_x, shape, 0, CX - PATCH + 1)
    along_y = jax.random.randint(key_y, shape, 0, CY - PATCH + 1)
    along_z = jax.random.randint(key_z, shape, 0, CZ - PATCH + 1)
    return jnp.concatenate([along_x, along_y, along_z], axis=0).astype(jnp.int32)


def block_scale(rng, shape, pieces, smallest, top_value):
    gain = 1.0
    for position, blocks in pieces:
        heights = jax.random.uniform(jax.random.fold_in(jax.random.fold_in(rng, 6), position), (blocks,), jnp.float32, smallest / len(pieces), top_value / len(pieces))
        gain = gain * jnp.repeat(jnp.exp(heights), shape[position] // blocks).reshape((-1,) + (1,) * (len(shape) - 1 - position))
    return gain


def routed_block(stream_key, own, number, rows, amount, top, limit, slope):
    sequence = jax.random.permutation(stream_key, amount)
    heavy_load, usual = shares(amount, rows * top, limit, slope, True), shares(amount, rows * top, limit, slope, False)
    places = jnp.arange(amount)

    def named(tallies, turn):
        used = int((tallies > 0).sum())
        fixed = max(1, used // 4)
        moved = fixed + (places - fixed + turn * (used - fixed)) % max(1, amount - fixed)
        return jnp.zeros((amount,), jnp.int32).at[sequence[jnp.where(places < fixed, places, moved)]].set(jnp.asarray(tallies, jnp.int32))

    tallies = jnp.where(number % 4 == 0, named(heavy_load, number // 4), named(usual, number - number // 4 - 1))
    mixed = jax.random.permutation(jax.random.fold_in(own, 3), amount)
    donor, taker = mixed[0:amount // 2 * 2:2], mixed[1:amount // 2 * 2:2]
    slack = jnp.minimum(tallies[donor] - 1, limit - tallies[taker]) // 2
    slack = jnp.where((donor == sequence[0]) | (taker == sequence[0]) | (tallies[taker] == 0), 0, jnp.maximum(slack, 0))
    moved = jax.random.randint(jax.random.fold_in(own, 4), (amount // 2,), 0, 1 << 20) % (slack + 1)
    tallies = tallies.at[donor].add(-moved).at[taker].add(moved)
    members = jnp.searchsorted(jnp.cumsum(tallies), jnp.arange(rows * top), side="right").astype(jnp.int32)
    listing = members.reshape(top, rows).T
    listing = listing[jax.random.permutation(jax.random.fold_in(own, 1), rows)]
    turn = jax.random.randint(jax.random.fold_in(own, 2), (rows, 1), 0, top)
    return jnp.take_along_axis(listing, (jnp.arange(top)[None, :] + turn) % top, axis=1)


def shares(amount, total, reach, lean, full):
    portions = [(1 << 20) // math.isqrt(rank ** lean) + 1 for rank in range(1, amount + 1)]
    largest = reach if full else min(reach, max(-(-total // amount), total * portions[0] // sum(portions)))
    least = 1 if total - largest >= amount - 1 else 0
    holding, spare = [largest] + [least] * (amount - 1), total - largest - least * (amount - 1)
    while spare > 0:
        movable = [i for i in range(1, amount) if holding[i] < largest] or [i for i in range(1, amount) if holding[i] < reach]
        mass, remaining = sum([portions[i] for i in movable]), spare
        for i in movable:
            extra = min(reach - holding[i], max(1, remaining * portions[i] // mass), spare)
            holding[i] = holding[i] + extra
            spare = spare - extra
    return np.array(holding)


def gaussian(rng, shape, width, limit, shards=(), kind=jnp.bfloat16):
    result = jax.random.normal(rng, shape, jnp.float32) * width
    if len(shards) > 0:
        result = block_scale(rng, shape, shards, -0.22, 0.18) * result
    return jnp.clip(result, min=-limit, max=limit).astype(kind)


def setup_inputs(seed: int = 0) -> dict:
    key_list = jax.random.split(jax.random.key(seed), 8)
    flow_field = gaussian(key_list[0], (CHAN, NX, NY, CZ), 1.0, 6.0, ((1, 8), (2, 16)), jnp.float32)
    patch_corners = draw_patch_corners(jax.random.fold_in(key_list[7], 71), 0)
    patch_learner_keys = jax.random.split(jax.random.fold_in(key_list[2], 1), BRICKS_X * (BRICKS_Y * PB) // PB)
    patch_learner_turns = jax.random.permutation(jax.random.fold_in(key_list[2], 3), BRICKS_X * (BRICKS_Y * PB) // PB)
    patch_learner = jax.vmap(lambda own, number: routed_block(jax.random.fold_in(key_list[2], 2), own, number, PB, BRICKS_Y, 1, CAP, 2))(patch_learner_keys, patch_learner_turns).reshape((BRICKS_X, BRICKS_Y * PB, 1))
    drag_target = gaussian(key_list[3], (3, BRICKS_X, BRICKS_Y * PB), 1.0, 6.0, ((1, 8), (2, 16)))
    embed_weight = gaussian(key_list[4], (FEAT, HID), FEAT ** -0.5, 0.375, (), jnp.float32)
    mixer_weight = gaussian(key_list[5], (HID, HID), HID ** -0.5, 0.25, (), jnp.float32)
    head_weight = gaussian(key_list[6], (3, HID), HID ** -0.5, 0.25, (), jnp.float32)
    return {"flow_field": flow_field, "patch_corners": patch_corners, "patch_learner": patch_learner, "drag_target": drag_target, "embed_weight": embed_weight, "mixer_weight": mixer_weight, "head_weight": head_weight}


KAPPA = 0.15
EPSILON = 1e-06

def cut_patch(volume, start_x, start_y, start_z, extent):
    anchor = jnp.zeros((), jnp.int32)
    return lax.dynamic_slice(volume, (anchor, start_x.astype(jnp.int32), start_y.astype(jnp.int32), start_z.astype(jnp.int32)), (volume.shape[0], extent, extent, extent))

def patch_tokens(patch, edge):
    channels = patch.shape[0]
    across = patch.shape[1] // edge
    blocks = patch.reshape(channels, across, edge, across, edge, across, edge)
    blocks = blocks.transpose(1, 3, 5, 0, 2, 4, 6)
    return blocks.reshape(across ** 3 * channels * edge ** 3)

def patch_rows(volume, starts_x, starts_y, starts_z, extent, edge):

    def single(corner_x, corner_y, corner_z):
        return patch_tokens(cut_patch(volume, corner_x, corner_y, corner_z, extent), edge).astype(jnp.bfloat16)
    return jax.vmap(single)(starts_x, starts_y, starts_z)

def place_table(learner, peers, depth):
    choose = (learner[:, None] == jnp.arange(peers, dtype=jnp.int32)[None, :]).astype(jnp.int32)
    earlier = jnp.cumsum(choose, axis=0) - choose
    within = lax.optimization_barrier(jnp.sum(earlier * choose, axis=1))
    target_slot = learner * depth + within
    return (jnp.arange(peers * depth, dtype=jnp.int32)[:, None] == target_slot[None, :]).astype(jnp.float32)

def gelu_slope(values):
    return jax.vjp(jax.nn.gelu, values)[1](jnp.ones_like(values))[0]

def closure_grads(rows, goals, embed_weight, mixer_weight, head_weight, early):
    count = rows.shape[0]
    features, hidden = embed_weight.shape
    per_patch = rows.shape[1] // features
    inputs = rows.reshape(count * per_patch, features)
    embed_half = embed_weight.astype(jnp.bfloat16)
    mixer_half = mixer_weight.astype(jnp.bfloat16)
    first_pre = jnp.dot(inputs, embed_half, preferred_element_type=jnp.float32)
    first_act = jax.nn.gelu(first_pre).astype(jnp.bfloat16)
    second_pre = jnp.dot(first_act, mixer_half, preferred_element_type=jnp.float32)
    pooled = lax.optimization_barrier(jnp.mean(jax.nn.gelu(second_pre).reshape(count, per_patch, hidden), axis=1))
    predicted = jnp.dot(pooled, head_weight.T, precision=lax.Precision.HIGHEST)
    misfit = 2.0 * (predicted - goals.astype(jnp.float32))
    grad_head = jnp.dot(misfit.T, pooled, precision=lax.Precision.HIGHEST)
    pooled_back = jnp.dot(misfit, head_weight, precision=lax.Precision.HIGHEST) / per_patch
    second_back = pooled_back[:, None, :] * gelu_slope(second_pre).reshape(count, per_patch, hidden)
    second_back = second_back.reshape(count * per_patch, hidden).astype(jnp.bfloat16)
    grad_mixer = lax.dot_general(first_act, second_back, (((0,), (0,)), ((), ())), preferred_element_type=jnp.float32)
    grad_head, grad_mixer = early(grad_head, grad_mixer)
    first_back = lax.dot_general(second_back, mixer_half, (((1,), (1,)), ((), ())), preferred_element_type=jnp.float32)
    first_grad = (first_back * gelu_slope(first_pre)).astype(jnp.bfloat16)
    grad_embed = lax.dot_general(inputs, first_grad, (((0,), (0,)), ((), ())), preferred_element_type=jnp.float32)
    return (predicted, grad_embed, grad_mixer, grad_head)

def normalized(gradient):
    return gradient / jnp.sqrt(jnp.mean(gradient * gradient) + EPSILON)

def unchanged(grad_head, grad_mixer):
    return (grad_head, grad_mixer)

def diffuse(flow_field):
    beside_all = jnp.roll(flow_field, 1, axis=1) + jnp.roll(flow_field, -1, axis=1)
    beside_all = beside_all + jnp.roll(flow_field, 1, axis=2) + jnp.roll(flow_field, -1, axis=2)
    vertical = jnp.pad(flow_field, ((0, 0), (0, 0), (0, 0), (1, 1)))
    beside_all = beside_all + vertical[..., 2:] + vertical[..., :-2]
    return flow_field + KAPPA * (beside_all - 6.0 * flow_field)

def reference(flow_field, patch_corners, patch_learner, drag_target, embed_weight, mixer_weight, head_weight):
    advanced_flow = diffuse(flow_field)
    bricks = BRICKS_X * BRICKS_Y
    corner_rows = patch_corners.reshape(3, bricks, PB).transpose(1, 0, 2)
    learner_rows = patch_learner.reshape(bricks, PB)
    goal_rows = drag_target.reshape(3, bricks, PB).transpose(1, 2, 0)
    indices = jnp.arange(bricks, dtype=jnp.int32)

    def one_brick(totals, inputs):
        index, corner, learner, goals = inputs
        brick_x = index // BRICKS_Y
        brick_y = index % BRICKS_Y
        rows = patch_rows(flow_field, corner[0] + brick_x * CX, corner[1] + brick_y * CY, corner[2], PATCH, CUBE)
        predicted, grad_embed, grad_mixer, grad_head = closure_grads(rows, goals, embed_weight, mixer_weight, head_weight, unchanged)
        place = place_table(learner, BRICKS_Y, CAP)
        slot_pred = jnp.dot(place, predicted, precision=lax.Precision.HIGHEST)
        return ((totals[0] + grad_embed, totals[1] + grad_mixer, totals[2] + grad_head), slot_pred)
    start = (jnp.zeros(embed_weight.shape, jnp.float32), jnp.zeros(mixer_weight.shape, jnp.float32), jnp.zeros(head_weight.shape, jnp.float32))
    totals, slot_preds = lax.scan(one_brick, start, (indices, corner_rows, learner_rows, goal_rows))
    slot_drag = slot_preds.reshape(BRICKS_X, BRICKS_Y, BRICKS_Y, CAP, 3).transpose(4, 0, 2, 1, 3)
    slot_drag = slot_drag.reshape(3, BRICKS_X, BRICKS_Y * BRICKS_Y * CAP)
    return (advanced_flow, slot_drag, normalized(totals[0]), normalized(totals[1]), normalized(totals[2]))
```

```python
import functools
import jax
import jax.numpy as jnp
from jax import lax
from jax.experimental import pallas as pl
from jax.experimental.pallas import tpu as pltpu
from jax.sharding import PartitionSpec as P

CHAN, CX, CY, CZ = 4, 32, 24, 256
PB, CAP, HID, FEAT = 32, 4, 512, 256
COLS = CHAN * CX * CY
SLAB = (CX + 2) * CY
BX, BY = 8, 16
MESH = pl.DeviceIdType.MESH
TILES = 8
KAPPA = 0.15
EPSILON = 1e-06
GELU_S = 0.7978845608028654
GELU_C = 0.044715
F32, BF16 = jnp.float32, jnp.bfloat16


def iota(shape, axis):
    return lax.broadcasted_iota(jnp.int32, shape, axis)


def gelu_and_slope(x):
    x2 = x * x
    t = jnp.tanh(x * (x2 * (GELU_S * GELU_C) + GELU_S))
    h = 0.5 * t + 0.5
    value = x * h
    return value, h + value * (1.0 - h) * (x2 * (6.0 * GELU_S * GELU_C) + 2.0 * GELU_S)


def load_flow(flow_ref, field, sems):
    copies = [
        pltpu.make_async_copy(
            flow_ref.at[pl.ds(CX * CY * c, CX * CY), pl.ds(128 * h, 128)],
            field.at[h, pl.ds(SLAB * c + CY, CX * CY)],
            sems.at[h, c],
        )
        for h in range(2)
        for c in range(CHAN)
    ]
    for copy in copies:
        copy.start()
    return copies


def level_of(field, h, y):
    return jnp.concatenate(
        [field[h, pl.ds(SLAB * c + CY + y, CX, stride=CY), :] for c in range(CHAN)], 0
    )


def upright(h, field, turned):
    for y in range(CY):
        turned[pl.ds(y * CZ + 128 * h, 128), :] = level_of(field, h, y).T


def cut(patches, corners_ref, turned, pieces):
    upper = iota((8, 128), 0) < 4
    even = iota((8, 128), 1) % 32 < 16
    for p in patches:
        x0, y0, z0 = corners_ref[0, 0, p], corners_ref[1, 0, p], corners_ref[2, 0, p]
        base = y0 * CZ + z0
        back = lax.rem(128 - x0, 128)
        for pair in range(8):
            halves = []
            for cy in (0, 2):
                both = []
                for parity in range(2):
                    fy, fz = divmod(2 * pair + parity, 4)
                    first = base + (4 * cy + fy) * CZ + fz
                    a = turned[pl.ds(first, 8, stride=4), :]
                    b = turned[pl.ds(first + 4 * CZ - 16, 8, stride=4), :]
                    both.append(
                        pltpu.roll(jnp.where(upper, a, b), back + 16 * parity, 1)
                    )
                halves.append(jnp.where(even, both[0], both[1]))
            pieces[pl.ds(16 * p, 16), pl.ds(128 * pair, 128)] = jnp.concatenate(halves, 0).astype(BF16)


def make_order(order):
    for block in range(8):
        k = iota((128, 1), 0)
        c, parity, cx, fx = k // 32, k // 16 % 2, k // 4 % 4, k % 4
        fyz = 2 * block + parity
        target = cx * FEAT + c * 64 + fx * 16 + fyz
        hit = iota((128, 4 * FEAT), 1) == target
        order[pl.ds(128 * block, 128), :] = jnp.where(hit, 1.0, 0.0).astype(BF16)


def order_rows(half, pieces, order, rows, rows_t):
    tiles = range(4 * half, 4 * half + 4)
    for cx in range(4):
        got = jnp.dot(
            pieces[pl.ds(256 * half, 256), :],
            order[:, pl.ds(FEAT * cx, FEAT)],
            preferred_element_type=F32,
        ).astype(BF16)
        for n, t in enumerate(tiles):
            rows[pl.ds(256 * t + 64 * cx, 64), :] = got[64 * n : 64 * n + 64]
    for t in tiles:
        rows_t[:, pl.ds(256 * t, 256)] = rows[pl.ds(256 * t, 256), :].T


def forward(t, rows, embed, mixer, act, act_t, slope1, slope2, pooled):
    at = pl.ds(t * 256, 256)
    for n in range(2):
        columns = pl.ds(256 * n, 256)
        pre = jnp.dot(rows[at, :], embed[:, columns], preferred_element_type=F32)
        value, slope = gelu_and_slope(pre)
        value = value.astype(BF16)
        act[at, columns] = value
        act_t[columns, at] = value.T
        slope1[at, columns] = slope
    for n in range(2):
        columns = pl.ds(256 * n, 256)
        pre = jnp.dot(act[at, :], mixer[:, columns], preferred_element_type=F32)
        value, slope = gelu_and_slope(pre)
        slope2[at, columns] = slope
        value = value.reshape(4, 4, 16, 256).sum(axis=0).sum(axis=1)
        pooled[t, :, columns] = value * (1.0 / 64)


def head_step(half, pooled_ref, goals_ref, learner_ref, head_ref, back, head_grad, slot_part):
    some = PB // 2
    first = some * half
    pooled = pooled_ref[pl.ds(4 * half, 4)].reshape(some, HID)
    head = head_ref[...]
    patch = iota((some, PB), 0) + first
    other = iota((some, PB), 1)
    learner_row = learner_ref[...]
    learner = jnp.sum(jnp.where(patch == other, learner_row, 0), axis=1, keepdims=True)
    earlier = (learner == learner_row) & (other < patch)
    within = jnp.sum(jnp.where(earlier, 1, 0), axis=1, keepdims=True)
    slot = learner * CAP + within
    place = iota((some, 128), 1) == slot
    total = jnp.zeros((some, HID), F32)
    head_rows, slot_rows = [], []
    for k in range(3):
        weight = head[k : k + 1, :]
        predicted = jnp.sum(pooled * weight, axis=1, keepdims=True)
        goal = goals_ref[k : k + 1, :].astype(F32)
        goal = jnp.sum(jnp.where(patch == other, goal, 0.0), axis=1, keepdims=True)
        misfit = 2.0 * (predicted - goal)
        total = total + misfit * weight
        head_rows.append(jnp.sum(misfit * pooled, axis=0, keepdims=True))
        slot_rows.append(jnp.sum(jnp.where(place, predicted, 0.0), axis=0, keepdims=True))
    back[pl.ds(4 * half, 4)] = (total * (1.0 / 64)).reshape(4, 4, HID)
    if half == 0:
        head_grad[...] = jnp.zeros_like(head_grad)
        slot_part[...] = jnp.zeros_like(slot_part)
    for k in range(3):
        head_grad[k : k + 1, :] += head_rows[k][:, 0:256]
        head_grad[k + 3 : k + 4, :] += head_rows[k][:, 256:512]
        slot_part[k : k + 1, :] += slot_rows[k]


def second_layer_back(t, back, slope2, second):
    at = pl.ds(t * 256, 256)
    for n in range(2):
        columns = pl.ds(256 * n, 256)
        slope = slope2[at, columns].reshape(4, 4, 16, 256)
        value = slope * back[t, :, columns][None, :, None, :]
        second[at, columns] = value.reshape(256, 256).astype(BF16)


def first_layer_back(t, second, mixer_t, slope1, first):
    at = pl.ds(t * 256, 256)
    for n in range(2):
        columns = pl.ds(256 * n, 256)
        value = jnp.dot(second[at, :], mixer_t[:, columns], preferred_element_type=F32)
        first[at, columns] = (value * slope1[at, columns]).astype(BF16)


def send_all(axis, source, target, send_sem, recv_sem):
    bx, by = lax.axis_index("bx"), lax.axis_index("by")
    me, size = (by, BY) if axis == "by" else (bx, BX)

    def step(distance, carry):
        peer = lax.rem(me + distance, size)
        pltpu.make_async_remote_copy(
            src_ref=source(peer),
            dst_ref=target,
            send_sem=send_sem,
            recv_sem=recv_sem,
            device_id=(bx, peer) if axis == "by" else (peer, by),
            device_id_type=MESH,
        ).start()
        return carry

    lax.fori_loop(1, size, step, 0)


def wait_all(buffer, sem):
    blocks = buffer.at[pl.ds(0, buffer.shape[0] - 1)]
    pltpu.make_async_copy(blocks, blocks, sem).wait()


def where_am_i():
    bx, by = lax.axis_index("bx"), lax.axis_index("by")
    div, rem = lax.div, lax.rem
    return [div(bx, 2), rem(div(by, 2), 4), div(by, 8) * 2 + rem(bx, 2), rem(by, 2)]


def device_at(place):
    x, y, z, core = place
    return (x * 2 + lax.rem(z, 2), lax.div(z, 2) * 8 + y * 2 + core)


PLANES = ((0, 1), (1, 2), (2, 0))
LINES = (2, 0, 1)


def plane_peers(job):
    place = where_am_i()
    first, second = PLANES[job]
    turns = [[lax.rem(place[axis] + d, 4) for d in range(4)] for axis in (first, second)]
    peers = []
    for d in (10, 6, 14, 9, 11, 2, 8, 5, 7, 13, 15, 1, 3, 4, 12, 0):
        for other in (0, 1) if job == 2 else (0,):
            if d == 0 and other == 0:
                continue
            there = list(place)
            there[first], there[second] = turns[0][d // 4], turns[1][d % 4]
            block = there[first] * 4 + there[second]
            if other:
                there[3] = 1 - place[3]
            if job == 2:
                block = block + 16 * there[3]
            peers.append((block, device_at(there)))
    return peers


def plane_index(job):
    place = where_am_i()
    first, second = PLANES[job]
    block = place[first] * 4 + place[second]
    return block + 16 * place[3] if job == 2 else block


def mate():
    place = where_am_i()
    place[3] = 1 - place[3]
    return device_at(place)


def partners():
    found = set()
    for y in range(4):
        for z in (0, 2):
            found.update((0, y, z, core) for core in (0, 1))
    for job in range(3):
        for d in range(16):
            there = [0, 0, 0, 0]
            there[PLANES[job][0]], there[PLANES[job][1]] = d // 4, d % 4
            for core in (0, 1) if job == 2 else (0,):
                there[3] = core
                found.add(tuple(there))
    return sorted(found - {(0, 0, 0, 0)})


def greet():
    barrier = pltpu.get_barrier_semaphore()
    here = where_am_i()
    turns = [[lax.rem(here[axis] + d, 4) for d in range(4)] for axis in range(3)]
    for x, y, z, core in partners():
        device = device_at((turns[0][x], turns[1][y], turns[2][z], 1 - here[3] if core else here[3]))
        pl.semaphore_signal(barrier, inc=1, device_id=device, device_id_type=MESH)


def send_plane(job, source, target, sems):
    for n, device in plane_peers(job):
        pltpu.make_async_remote_copy(
            src_ref=source(n),
            dst_ref=target,
            send_sem=sems[0],
            recv_sem=sems[1],
            device_id=device,
            device_id_type=MESH,
        ).start()


def send_line(axis, block, sems):
    for distance in (2, 1, 3):
        place = where_am_i()
        place[axis] = lax.rem(place[axis] + distance, 4)
        pltpu.make_async_remote_copy(
            src_ref=block,
            dst_ref=block,
            send_sem=sems[0],
            recv_sem=sems[1],
            device_id=device_at(place),
            device_id_type=MESH,
        ).start()


def send_mate(source, target, sems):
    pltpu.make_async_remote_copy(
        src_ref=source,
        dst_ref=target,
        send_sem=sems[0],
        recv_sem=sems[1],
        device_id=mate(),
        device_id_type=MESH,
    ).start()


def wait_one(buffer, sem):
    pltpu.make_async_copy(buffer, buffer, sem).wait()


def fill_faces(field, x_face, y_face):
    for h in range(2):
        for side, x in ((0, 0), (1, CX - 1)):
            layers = [field[h, pl.ds(SLAB * c + CY * (x + 1), CY), :] for c in range(CHAN)]
            x_face[side, h] = jnp.concatenate(layers, 0).astype(BF16)
        for side, y in ((0, 0), (1, CY - 1)):
            y_face[side, h] = level_of(field, h, y).astype(BF16)


def halo_copies(x_face, y_face, x_halo, y_halo, send_sems, recv_sems):
    bx, by = lax.axis_index("bx"), lax.axis_index("by")
    copies = []
    for n, (face, halo, device) in enumerate(
        (
            (x_face.at[1], x_halo.at[0], (lax.rem(bx + 1, BX), by)),
            (x_face.at[0], x_halo.at[1], (lax.rem(bx + BX - 1, BX), by)),
            (y_face.at[1], y_halo.at[0], (bx, lax.rem(by + 1, BY))),
            (y_face.at[0], y_halo.at[1], (bx, lax.rem(by + BY - 1, BY))),
        )
    ):
        copies.append(
            pltpu.make_async_remote_copy(
                src_ref=face,
                dst_ref=halo,
                send_sem=send_sems.at[n],
                recv_sem=recv_sems.at[n],
                device_id=device,
                device_id_type=MESH,
            )
        )
    return copies


def place_halos(x_halo, y_halo, field, y_edge):
    for h in range(2):
        for side, slot in ((0, 0), (1, CX + 1)):
            layers = x_halo[side, h].astype(F32)
            for c in range(CHAN):
                rows = pl.ds(SLAB * c + CY * slot, CY)
                field[h, rows, :] = layers[CY * c : CY * c + CY]
            y_edge[side, h] = y_halo[side, h].astype(F32)


def diffuse(c, field, y_edge, moved):
    row, lane = iota((CY, 128), 0), iota((CY, 128), 1)

    def column(x, carry):
        first = SLAB * c + CY + CY * x
        here = pl.ds(pl.multiple_of(first, 8), CY)
        cells = [field[h, here, :] for h in range(2)]
        down = [pltpu.roll(cells[h], 1, 1) for h in range(2)]
        up = [pltpu.roll(cells[h], 127, 1) for h in range(2)]
        below = [jnp.where(lane == 0, 0.0, down[0]), jnp.where(lane == 0, down[0], down[1])]
        above = [jnp.where(lane == 127, up[1], up[0]), jnp.where(lane == 127, 0.0, up[1])]
        for h in range(2):
            total = below[h] + above[h]
            total = total + field[h, pl.ds(pl.multiple_of(first - CY, 8), CY), :]
            total = total + field[h, pl.ds(pl.multiple_of(first + CY, 8), CY), :]
            low = y_edge[0, h, pl.ds(CX * c + x, 1), :]
            high = y_edge[1, h, pl.ds(CX * c + x, 1), :]
            total = total + jnp.where(row == 0, low, field[h, pl.ds(first - 1, CY), :])
            total = total + jnp.where(row == CY - 1, high, field[h, pl.ds(first + 1, CY), :])
            rows = pl.ds(pl.multiple_of(CX * CY * c + CY * x, 8), CY)
            moved[h, rows, :] = (1.0 - 6.0 * KAPPA) * cells[h] + KAPPA * total
        return carry

    lax.fori_loop(0, CX, column, 0, unroll=8)


def sum_blocks(buffer, count):
    total = buffer[0].astype(F32)
    for n in range(1, count):
        total = total + buffer[n].astype(F32)
    return total


def read_slots(slot_got):
    by = lax.axis_index("by")
    lane = iota((8, 128), 1)
    total = jnp.zeros((8, 128), F32)
    for j in range(BY):
        block = pltpu.roll(slot_got[j], lax.rem(128 + CAP * j - CAP * by, 128), 1)
        total = jnp.where(lane // CAP == j, block, total)
    return total


PAIR, PLANE, LINE, PLANE_ALL, MATE = range(5)


def step_kernel(
    corners_ref, flow_ref, learner_ref, goals_ref, embed_ref, mixer_ref, head_ref,
    moved, full, full_e, head_total, slots,
    field, turned, pieces, order, rows, embed_wide, mixer_wide, embed, mixer, mixer_t, act, slope1,
    slope2, pooled, back, second, first, rows_t, act_t, mixer_early, x_face, y_face, x_halo, y_halo, y_edge,
    head_grad, head_pair, head_got, slot_part, slot_got, own, pair_got, part, plane_got, line_got, part_e, plane_got_e,
    load_sems, weight_sems, halo_send, halo_recv, slot_sems, head_send, head_recv, job_send, job_recv,
):
    bx, by = lax.axis_index("bx"), lax.axis_index("by")
    core = lax.rem(by, 2)
    loads = load_flow(flow_ref, field, load_sems)
    weights = [
        pltpu.make_async_copy(embed_ref, embed_wide, weight_sems.at[0]),
        pltpu.make_async_copy(mixer_ref, mixer_wide, weight_sems.at[1]),
    ]
    for copy in weights:
        copy.start()
    greet()
    make_order(order)
    for h in range(2):
        for c in range(CHAN):
            loads[h * CHAN + c].wait()
        upright(h, field, turned)
    early, late = pl.ds(0, 1024), pl.ds(1024, 1024)

    def product(turned_rows, columns, along, factor):
        return jnp.dot(turned_rows[columns, along], factor[along, :], preferred_element_type=F32)

    cut(range(0, 16), corners_ref, turned, pieces)
    for copy in weights:
        copy.wait()
    order_rows(0, pieces, order, rows, rows_t)
    embed[...] = embed_wide[...].astype(BF16)
    mixer[...] = mixer_wide[...].astype(BF16)
    mixer_t[...] = mixer_wide[...].T.astype(BF16)
    fill_faces(field, x_face, y_face)
    pl.semaphore_wait(pltpu.get_barrier_semaphore(), len(partners()))
    halos = halo_copies(x_face, y_face, x_halo, y_halo, halo_send, halo_recv)
    for copy in halos:
        copy.start()
    for t in range(4):
        forward(t, rows, embed, mixer, act, act_t, slope1, slope2, pooled)
        cut(range(16 + 4 * t, 20 + 4 * t), corners_ref, turned, pieces)
    order_rows(1, pieces, order, rows, rows_t)
    head_step(0, pooled, goals_ref, learner_ref, head_ref, back, head_grad, slot_part)
    for t in range(4, 8):
        forward(t, rows, embed, mixer, act, act_t, slope1, slope2, pooled)
        second_layer_back(t - 4, back, slope2, second)
    head_step(1, pooled, goals_ref, learner_ref, head_ref, back, head_grad, slot_part)
    for half in range(2):
        part_of = pl.ds(256 * half, 256)
        mixer_early[part_of, :] = product(act_t, part_of, early, second)

    send_all("by", lambda peer: slot_part, slot_got.at[by], slot_sems.at[0], slot_sems.at[1])
    slot_got[by] = slot_part[...]
    send_mate(head_grad, head_pair, (head_send.at[0], head_recv.at[0]))

    def head_line(axis, value):
        me = where_am_i()[axis]
        block = head_got.at[axis, me]
        block[...] = value
        send_line(axis, block, (head_send.at[axis + 1], head_recv.at[axis + 1]))

    def head_line_sum(axis):
        wait_all(head_got.at[axis], head_recv.at[axis + 1])
        return sum_blocks(head_got.at[axis], 4)

    def sems(job, group):
        return job_send.at[job, group], job_recv.at[job, group]

    def start_pair(job, gradient):
        own[job] = gradient.reshape(2, 128, HID).astype(BF16)
        send_mate(own.at[job, 1 - core], pair_got.at[job], sems(job, PAIR))

    parts = (part.at[0], part.at[1], part_e)
    gots = (plane_got.at[0], plane_got.at[1], plane_got_e)
    fulls = (full.at[0, core], full.at[1, core], full_e)

    def plane_sends(job):
        me = plane_index(job)
        send_plane(job, lambda n: parts[job].at[n], gots[job].at[me], sems(job, PLANE))
        gots[job][me] = parts[job][me]

    def start_plane(job):
        wait_one(pair_got.at[job], job_recv.at[job, PAIR])
        total = (own[job, core].astype(F32) + pair_got[job].astype(F32)).astype(BF16)
        for n in range(16):
            part[job, n] = total[16 * (n // 2) : 16 * (n // 2) + 16, 256 * (n % 2) : 256 * (n % 2) + 256]
        plane_sends(job)

    def start_plane_e(gradient):
        total = gradient.astype(BF16)
        for n in range(32):
            part_e[n] = total[16 * (n // 2) : 16 * (n // 2) + 16, 256 * (n % 2) : 256 * (n % 2) + 256]
        plane_sends(2)

    def start_line(job):
        wait_all(gots[job], job_recv.at[job, PLANE])
        me = where_am_i()[LINES[job]]
        line_got[job, me] = sum_blocks(gots[job], gots[job].shape[0]).astype(BF16)
        send_line(LINES[job], line_got.at[job, me], sems(job, LINE))

    def start_plane_all(job):
        wait_all(line_got.at[job], job_recv.at[job, LINE])
        block = fulls[job].at[plane_index(job)]
        block[...] = sum_blocks(line_got.at[job], 4).astype(BF16)
        send_plane(job, lambda n: block, block, sems(job, PLANE_ALL))

    def start_mate(job):
        wait_all(fulls[job], job_recv.at[job, PLANE_ALL])
        send_mate(fulls[job], fulls[job], sems(job, MATE))

    for t in range(4, 8):
        second_layer_back(t, back, slope2, second)
    for half in range(2):
        part_of = pl.ds(256 * half, 256)
        start_pair(half, mixer_early[part_of, :] + product(act_t, part_of, late, second))
    for t in range(TILES):
        first_layer_back(t, second, mixer_t, slope1, first)
    start_plane(0)
    start_plane(1)
    start_plane_e(jnp.dot(rows_t[...], first[...], preferred_element_type=F32))

    wait_one(head_pair, head_recv.at[0])
    head_line(1, head_grad[...] + head_pair[...])
    for copy in halos:
        copy.wait()
    place_halos(x_halo, y_halo, field, y_edge)
    start_line(0)
    start_line(1)
    head_line(2, head_line_sum(1))
    diffuse(0, field, y_edge, moved)
    start_plane_all(0)
    start_plane_all(1)
    start_line(2)
    head_line(0, head_line_sum(2))
    diffuse(1, field, y_edge, moved)
    start_plane_all(2)
    wait_all(slot_got, slot_sems.at[1])
    slots[...] = read_slots(slot_got)
    diffuse(2, field, y_edge, moved)
    start_mate(0)
    start_mate(1)
    diffuse(3, field, y_edge, moved)
    head_total[...] = head_line_sum(0)
    wait_all(full_e, job_recv.at[2, PLANE_ALL])
    for job in range(2):
        wait_one(full.at[job, 1 - core], job_recv.at[job, MATE])
    wait_all(slot_got, slot_sems.at[0])
    wait_one(head_pair, head_send.at[0])
    for axis in range(3):
        wait_all(head_got.at[axis], head_send.at[axis + 1])
    for job in range(3):
        wait_all(gots[job], job_send.at[job, PLANE])
        wait_all(line_got.at[job], job_send.at[job, LINE])
        wait_all(fulls[job], job_send.at[job, PLANE_ALL])
    for job in range(2):
        wait_one(pair_got.at[job], job_send.at[job, PAIR])
        wait_one(fulls[job], job_send.at[job, MATE])


def scale_of(square_sum, count):
    return lax.rsqrt(jnp.sum(square_sum, keepdims=True) * (1.0 / count) + EPSILON)


def write_sum(blocks, wide, out, sems):
    total = jnp.zeros((16, 256), F32)
    for block in blocks:
        value = block[...].astype(F32)
        total = total + value * value
    scale = scale_of(total, len(blocks) * 16 * 256)
    copies = []
    for n, block in enumerate(blocks):
        wide[pl.ds(16 * (n // 2), 16), pl.ds(256 * (n % 2), 256)] = block[...].astype(F32) * scale
        if n % 16 == 15:
            rows = pl.ds(128 * (n // 16), 128)
            copies.append(pltpu.make_async_copy(wide.at[rows], out.at[rows], sems.at[n // 16]))
            copies[-1].start()
    return copies


def finish_kernel(
    moved, full, full_e, head_total, slots, flow_out, slot_out, embed_out, mixer_out, head_out,
    embed_wide, mixer_wide, flow_sems, embed_sems, mixer_sems,
):
    copies = []
    for c in range(CHAN):
        part = pl.ds(CX * CY * c, CX * CY)
        for h in range(2):
            copies.append(
                pltpu.make_async_copy(
                    moved.at[h, part], flow_out.at[part, pl.ds(128 * h, 128)], flow_sems.at[h, c]
                )
            )
    for copy in copies:
        copy.start()
    copies += write_sum(
        [full.at[j, h, n] for j in range(2) for h in range(2) for n in range(16)],
        mixer_wide, mixer_out, mixer_sems,
    )
    copies += write_sum([full_e.at[n] for n in range(32)], embed_wide, embed_out, embed_sems)
    total = head_total[...]
    total = total * scale_of(total * total, 3 * HID)
    for k in range(3):
        head_out[k : k + 1, 0:256] = total[k : k + 1]
        head_out[k : k + 1, 256:512] = total[k + 3 : k + 4]
        slot_out[k] = slots[k : k + 1, 0:64]
    for copy in copies:
        copy.wait()


SCRATCH = [
    pltpu.VMEM((2, CHAN * SLAB, 128), F32),
    pltpu.VMEM((CY * CZ + 32, 128), F32),
    pltpu.VMEM((512, 1024), BF16),
    pltpu.VMEM((1024, 1024), BF16),
    pltpu.VMEM((2048, FEAT), BF16),
    pltpu.VMEM((FEAT, HID), F32),
    pltpu.VMEM((HID, HID), F32),
    pltpu.VMEM((FEAT, HID), BF16),
    pltpu.VMEM((HID, HID), BF16),
    pltpu.VMEM((HID, HID), BF16),
    pltpu.VMEM((2048, HID), BF16),
    pltpu.VMEM((2048, HID), F32),
    pltpu.VMEM((2048, HID), F32),
    pltpu.VMEM((TILES, 4, HID), F32),
    pltpu.VMEM((TILES, 4, HID), F32),
    pltpu.VMEM((2048, HID), BF16),
    pltpu.VMEM((2048, HID), BF16),
    pltpu.VMEM((FEAT, 2048), BF16),
    pltpu.VMEM((HID, 2048), BF16),
    pltpu.VMEM((HID, HID), F32),
    pltpu.VMEM((2, 2, CHAN * CY, 128), BF16),
    pltpu.VMEM((2, 2, CHAN * CX, 128), BF16),
    pltpu.VMEM((2, 2, CHAN * CY, 128), BF16),
    pltpu.VMEM((2, 2, CHAN * CX, 128), BF16),
    pltpu.VMEM((2, 2, CHAN * CX, 128), F32),
    pltpu.VMEM((8, 256), F32),
    pltpu.VMEM((8, 256), F32),
    pltpu.VMEM((3, 4, 8, 256), F32),
    pltpu.VMEM((8, 128), F32),
    pltpu.VMEM((BY, 8, 128), F32),
    pltpu.VMEM((2, 2, 128, HID), BF16),
    pltpu.VMEM((2, 128, HID), BF16),
    pltpu.VMEM((2, 16, 16, 256), BF16),
    pltpu.VMEM((2, 16, 16, 256), BF16),
    pltpu.VMEM((3, 4, 16, 256), BF16),
    pltpu.VMEM((32, 16, 256), BF16),
    pltpu.VMEM((32, 16, 256), BF16),
    pltpu.SemaphoreType.DMA((2, CHAN)),
    pltpu.SemaphoreType.DMA((2,)),
    pltpu.SemaphoreType.DMA((4,)),
    pltpu.SemaphoreType.DMA((4,)),
    pltpu.SemaphoreType.DMA((2,)),
    pltpu.SemaphoreType.DMA((4,)),
    pltpu.SemaphoreType.DMA((4,)),
    pltpu.SemaphoreType.DMA((3, 5)),
    pltpu.SemaphoreType.DMA((3, 5)),
]


def per_device(
    flow_field, patch_corners, patch_learner, drag_target, embed_weight, mixer_weight, head_weight
):
    vmem = pl.BlockSpec(memory_space=pltpu.VMEM)
    anywhere = pl.BlockSpec(memory_space=pl.ANY)
    parts = pl.pallas_call(
        step_kernel,
        out_shape=(
            pltpu.VMEM((2, COLS, 128), F32),
            pltpu.VMEM((2, 2, 16, 16, 256), BF16),
            pltpu.VMEM((32, 16, 256), BF16),
            pltpu.VMEM((8, 256), F32),
            pltpu.VMEM((8, 128), F32),
        ),
        in_specs=[pl.BlockSpec(memory_space=pltpu.SMEM), anywhere, vmem, vmem, anywhere, anywhere, vmem],
        out_specs=(vmem,) * 5,
        scratch_shapes=SCRATCH,
        compiler_params=pltpu.CompilerParams(
            collective_id=0, has_side_effects=True, vmem_limit_bytes=44 * 2**20
        ),
    )(
        *(
            pltpu.with_memory_space_constraint(value, pltpu.HBM)
            for value in (
                patch_corners, flow_field.reshape(COLS, CZ), patch_learner.reshape(1, PB),
                drag_target.reshape(3, PB), embed_weight, mixer_weight, head_weight,
            )
        )
    )
    flow, slots, embed, mixer, head = pl.pallas_call(
        finish_kernel,
        out_shape=(
            jax.ShapeDtypeStruct((COLS, CZ), F32),
            jax.ShapeDtypeStruct((3, 1, 64), F32),
            jax.ShapeDtypeStruct((FEAT, HID), F32),
            jax.ShapeDtypeStruct((HID, HID), F32),
            jax.ShapeDtypeStruct((3, HID), F32),
        ),
        in_specs=[vmem] * 5,
        out_specs=(anywhere, vmem, anywhere, anywhere, vmem),
        scratch_shapes=[
            pltpu.VMEM((FEAT, HID), F32),
            pltpu.VMEM((HID, HID), F32),
            pltpu.SemaphoreType.DMA((2, CHAN)),
            pltpu.SemaphoreType.DMA((2,)),
            pltpu.SemaphoreType.DMA((4,)),
        ],
        compiler_params=pltpu.CompilerParams(vmem_limit_bytes=16 * 2**20),
    )(*parts)
    return flow.reshape(CHAN, CX, CY, CZ), slots, embed, mixer, head


def solution(mesh):
    return jax.shard_map(
        per_device,
        mesh=mesh,
        in_specs=(
            P(None, "bx", "by", None),
            P(None, "bx", "by"),
            P("bx", "by", None),
            P(None, "bx", "by"),
            P(),
            P(),
            P(),
        ),
        out_specs=(P(None, "bx", "by", None), P(None, "bx", "by"), P(), P(), P()),
        check_vma=False,
    )
```

```python
import functools
import jax
import jax.numpy as jnp
from jax import lax
from jax.experimental import pallas as pl
from jax.experimental.pallas import tpu as pltpu
from jax.sharding import PartitionSpec as P

CHAN, CX, CY, CZ = 4, 32, 24, 256
PB, CAP, HID, FEAT = 32, 4, 512, 256
COLS = CHAN * CX * CY
SLAB = (CX + 2) * CY
BX, BY = 8, 16
MESH = pl.DeviceIdType.MESH
TILES = 8
KAPPA = 0.15
EPSILON = 1e-06
GELU_S = 0.7978845608028654
GELU_C = 0.044715
F32, BF16 = jnp.float32, jnp.bfloat16


def iota(shape, axis):
    return lax.broadcasted_iota(jnp.int32, shape, axis)


def gelu_and_slope(x):
    x2 = x * x
    t = jnp.tanh(x * (x2 * (GELU_S * GELU_C) + GELU_S))
    h = 0.5 * t + 0.5
    value = x * h
    return value, h + value * (1.0 - h) * (x2 * (6.0 * GELU_S * GELU_C) + 2.0 * GELU_S)


def load_flow(flow_ref, field, sems):
    cells = field.reshape(2, CHAN * (CX + 2), CY, 128)

    def copy(block, h, c):
        levels = pl.ds(8 * block, 8)
        return pltpu.make_async_copy(
            flow_ref.at[pl.ds(CX * c, CX), levels, pl.ds(128 * h, 128)],
            cells.at[h, pl.ds((CX + 2) * c + 1, CX), levels],
            sems.at[block, h, c],
        )

    copies = [[[copy(block, h, c) for c in range(CHAN)] for h in range(2)] for block in range(3)]
    for copy in sum(sum(copies, []), []):
        copy.start()
    return copies


def level_of(field, h, y):
    return jnp.concatenate(
        [field[h, pl.ds(SLAB * c + CY + y, CX, stride=CY), :] for c in range(CHAN)], 0
    )


def upright(block, h, field, turned):
    for y in range(8 * block, 8 * block + 8):
        turned[pl.ds(y * CZ + 128 * h, 128), :] = level_of(field, h, y).T


def cut(patches, corners_ref, turned, pieces):
    upper = iota((8, 128), 0) < 4
    even = iota((8, 128), 1) % 32 < 16
    for p in patches:
        x0, y0, z0 = corners_ref[0, 0, p], corners_ref[1, 0, p], corners_ref[2, 0, p]
        base = y0 * CZ + z0
        back = lax.rem(128 - x0, 128)
        for pair in range(8):
            halves = []
            for cy in (0, 2):
                both = []
                for parity in range(2):
                    fy, fz = divmod(2 * pair + parity, 4)
                    first = base + (4 * cy + fy) * CZ + fz
                    a = turned[pl.ds(first, 8, stride=4), :]
                    b = turned[pl.ds(first + 4 * CZ - 16, 8, stride=4), :]
                    both.append(
                        pltpu.roll(jnp.where(upper, a, b), back + 16 * parity, 1)
                    )
                halves.append(jnp.where(even, both[0], both[1]))
            pieces[pl.ds(16 * p, 16), pl.ds(128 * pair, 128)] = jnp.concatenate(halves, 0).astype(BF16)


def make_order(order):
    for block in range(8):
        k = iota((128, 1), 0)
        c, parity, cx, fx = k // 32, k // 16 % 2, k // 4 % 4, k % 4
        fyz = 2 * block + parity
        target = cx * FEAT + c * 64 + fx * 16 + fyz
        hit = iota((128, 4 * FEAT), 1) == target
        order[pl.ds(128 * block, 128), :] = jnp.where(hit, 1.0, 0.0).astype(BF16)


def order_rows(half, pieces, order, rows, rows_t):
    tiles = range(4 * half, 4 * half + 4)
    for cx in range(4):
        got = jnp.dot(
            pieces[pl.ds(256 * half, 256), :],
            order[:, pl.ds(FEAT * cx, FEAT)],
            preferred_element_type=F32,
        ).astype(BF16)
        for n, t in enumerate(tiles):
            rows[pl.ds(256 * t + 64 * cx, 64), :] = got[64 * n : 64 * n + 64]
    for t in tiles:
        rows_t[:, pl.ds(256 * t, 256)] = rows[pl.ds(256 * t, 256), :].T


def forward(t, rows, embed, mixer, act, act_t, slope1, slope2, pooled):
    at = pl.ds(t * 256, 256)
    for n in range(2):
        columns = pl.ds(256 * n, 256)
        pre = jnp.dot(rows[at, :], embed[:, columns], preferred_element_type=F32)
        value, slope = gelu_and_slope(pre)
        value = value.astype(BF16)
        act[at, columns] = value
        act_t[columns, at] = value.T
        slope1[at, columns] = slope
    for n in range(2):
        columns = pl.ds(256 * n, 256)
        pre = jnp.dot(act[at, :], mixer[:, columns], preferred_element_type=F32)
        value, slope = gelu_and_slope(pre)
        slope2[at, columns] = slope
        value = value.reshape(4, 4, 16, 256).sum(axis=0).sum(axis=1)
        pooled[t, :, columns] = value * (1.0 / 64)


def head_step(half, pooled_ref, goals_ref, learner_ref, head_ref, back, head_grad, slot_part):
    some = PB // 2
    first = some * half
    pooled = pooled_ref[pl.ds(4 * half, 4)].reshape(some, HID)
    head = head_ref[...]
    patch = iota((some, PB), 0) + first
    other = iota((some, PB), 1)
    learner_row = learner_ref[...]
    learner = jnp.sum(jnp.where(patch == other, learner_row, 0), axis=1, keepdims=True)
    earlier = (learner == learner_row) & (other < patch)
    within = jnp.sum(jnp.where(earlier, 1, 0), axis=1, keepdims=True)
    slot = learner * CAP + within
    place = iota((some, 128), 1) == slot
    total = jnp.zeros((some, HID), F32)
    head_rows, slot_rows = [], []
    for k in range(3):
        weight = head[k : k + 1, :]
        predicted = jnp.sum(pooled * weight, axis=1, keepdims=True)
        goal = goals_ref[k : k + 1, :].astype(F32)
        goal = jnp.sum(jnp.where(patch == other, goal, 0.0), axis=1, keepdims=True)
        misfit = 2.0 * (predicted - goal)
        total = total + misfit * weight
        head_rows.append(jnp.sum(misfit * pooled, axis=0, keepdims=True))
        slot_rows.append(jnp.sum(jnp.where(place, predicted, 0.0), axis=0, keepdims=True))
    back[pl.ds(4 * half, 4)] = (total * (1.0 / 64)).reshape(4, 4, HID)
    if half == 0:
        head_grad[...] = jnp.zeros_like(head_grad)
        slot_part[...] = jnp.zeros_like(slot_part)
    for k in range(3):
        head_grad[k : k + 1, :] += head_rows[k][:, 0:256]
        head_grad[k + 3 : k + 4, :] += head_rows[k][:, 256:512]
        slot_part[k : k + 1, :] += slot_rows[k]


def second_layer_back(t, back, slope2, second):
    at = pl.ds(t * 256, 256)
    for n in range(2):
        columns = pl.ds(256 * n, 256)
        slope = slope2[at, columns].reshape(4, 4, 16, 256)
        value = slope * back[t, :, columns][None, :, None, :]
        second[at, columns] = value.reshape(256, 256).astype(BF16)


def first_layer_back(t, second, mixer_t, slope1, first):
    at = pl.ds(t * 256, 256)
    for n in range(2):
        columns = pl.ds(256 * n, 256)
        value = jnp.dot(second[at, :], mixer_t[:, columns], preferred_element_type=F32)
        first[at, columns] = (value * slope1[at, columns]).astype(BF16)


def send_all(axis, source, target, send_sem, recv_sem):
    bx, by = lax.axis_index("bx"), lax.axis_index("by")
    me, size = (by, BY) if axis == "by" else (bx, BX)

    def step(distance, carry):
        peer = lax.rem(me + distance, size)
        pltpu.make_async_remote_copy(
            src_ref=source(peer),
            dst_ref=target,
            send_sem=send_sem,
            recv_sem=recv_sem,
            device_id=(bx, peer) if axis == "by" else (peer, by),
            device_id_type=MESH,
        ).start()
        return carry

    lax.fori_loop(1, size, step, 0)


def wait_all(buffer, sem):
    blocks = buffer.at[pl.ds(0, buffer.shape[0] - 1)]
    pltpu.make_async_copy(blocks, blocks, sem).wait()


def where_am_i():
    bx, by = lax.axis_index("bx"), lax.axis_index("by")
    div, rem = lax.div, lax.rem
    return [div(bx, 2), rem(div(by, 2), 4), div(by, 8) * 2 + rem(bx, 2), rem(by, 2)]


def device_at(place):
    x, y, z, core = place
    return (x * 2 + lax.rem(z, 2), lax.div(z, 2) * 8 + y * 2 + core)


PLANES = ((0, 1), (1, 2), (2, 0))
LINES = (2, 0, 1)


def plane_peers(job):
    place = where_am_i()
    first, second = PLANES[job]
    turns = [[lax.rem(place[axis] + d, 4) for d in range(4)] for axis in (first, second)]
    peers = []
    for d in (10, 6, 14, 9, 11, 2, 8, 5, 7, 13, 15, 1, 3, 4, 12, 0):
        for other in (0, 1) if job == 2 else (0,):
            if d == 0 and other == 0:
                continue
            there = list(place)
            there[first], there[second] = turns[0][d // 4], turns[1][d % 4]
            block = there[first] * 4 + there[second]
            if other:
                there[3] = 1 - place[3]
            if job == 2:
                block = block + 16 * there[3]
            peers.append((block, device_at(there)))
    return peers


def plane_index(job):
    place = where_am_i()
    first, second = PLANES[job]
    block = place[first] * 4 + place[second]
    return block + 16 * place[3] if job == 2 else block


def mate():
    place = where_am_i()
    place[3] = 1 - place[3]
    return device_at(place)


def partners():
    found = set()
    for y in range(4):
        for z in (0, 2):
            found.update((0, y, z, core) for core in (0, 1))
    for job in range(3):
        for d in range(16):
            there = [0, 0, 0, 0]
            there[PLANES[job][0]], there[PLANES[job][1]] = d // 4, d % 4
            for core in (0, 1) if job == 2 else (0,):
                there[3] = core
                found.add(tuple(there))
    return sorted(found - {(0, 0, 0, 0)})


def greet():
    barrier = pltpu.get_barrier_semaphore()
    here = where_am_i()
    turns = [[lax.rem(here[axis] + d, 4) for d in range(4)] for axis in range(3)]
    for x, y, z, core in partners():
        device = device_at((turns[0][x], turns[1][y], turns[2][z], 1 - here[3] if core else here[3]))
        pl.semaphore_signal(barrier, inc=1, device_id=device, device_id_type=MESH)


def send_plane(job, source, target, sems):
    for n, device in plane_peers(job):
        pltpu.make_async_remote_copy(
            src_ref=source(n),
            dst_ref=target,
            send_sem=sems[0],
            recv_sem=sems[1],
            device_id=device,
            device_id_type=MESH,
        ).start()


def send_line(axis, block, sems):
    for distance in (2, 1, 3):
        place = where_am_i()
        place[axis] = lax.rem(place[axis] + distance, 4)
        pltpu.make_async_remote_copy(
            src_ref=block,
            dst_ref=block,
            send_sem=sems[0],
            recv_sem=sems[1],
            device_id=device_at(place),
            device_id_type=MESH,
        ).start()


def send_mate(source, target, sems):
    pltpu.make_async_remote_copy(
        src_ref=source,
        dst_ref=target,
        send_sem=sems[0],
        recv_sem=sems[1],
        device_id=mate(),
        device_id_type=MESH,
    ).start()


def wait_one(buffer, sem):
    pltpu.make_async_copy(buffer, buffer, sem).wait()


def fill_faces(field, x_face, y_face):
    for h in range(2):
        for side, x in ((0, 0), (1, CX - 1)):
            layers = [field[h, pl.ds(SLAB * c + CY * (x + 1), CY), :] for c in range(CHAN)]
            x_face[side, h] = jnp.concatenate(layers, 0).astype(BF16)
        for side, y in ((0, 0), (1, CY - 1)):
            y_face[side, h] = level_of(field, h, y).astype(BF16)


def halo_copies(x_face, y_face, x_halo, y_halo, send_sems, recv_sems):
    bx, by = lax.axis_index("bx"), lax.axis_index("by")
    copies = []
    for n, (face, halo, device) in enumerate(
        (
            (x_face.at[1], x_halo.at[0], (lax.rem(bx + 1, BX), by)),
            (x_face.at[0], x_halo.at[1], (lax.rem(bx + BX - 1, BX), by)),
            (y_face.at[1], y_halo.at[0], (bx, lax.rem(by + 1, BY))),
            (y_face.at[0], y_halo.at[1], (bx, lax.rem(by + BY - 1, BY))),
        )
    ):
        copies.append(
            pltpu.make_async_remote_copy(
                src_ref=face,
                dst_ref=halo,
                send_sem=send_sems.at[n],
                recv_sem=recv_sems.at[n],
                device_id=device,
                device_id_type=MESH,
            )
        )
    return copies


def place_halos(x_halo, y_halo, field, y_edge):
    for h in range(2):
        for side, slot in ((0, 0), (1, CX + 1)):
            layers = x_halo[side, h].astype(F32)
            for c in range(CHAN):
                rows = pl.ds(SLAB * c + CY * slot, CY)
                field[h, rows, :] = layers[CY * c : CY * c + CY]
            y_edge[side, h] = y_halo[side, h].astype(F32)


def diffuse(c, field, y_edge, moved):
    row, lane = iota((CY, 128), 0), iota((CY, 128), 1)

    def column(x, carry):
        first = SLAB * c + CY + CY * x
        here = pl.ds(pl.multiple_of(first, 8), CY)
        cells = [field[h, here, :] for h in range(2)]
        down = [pltpu.roll(cells[h], 1, 1) for h in range(2)]
        up = [pltpu.roll(cells[h], 127, 1) for h in range(2)]
        below = [jnp.where(lane == 0, 0.0, down[0]), jnp.where(lane == 0, down[0], down[1])]
        above = [jnp.where(lane == 127, up[1], up[0]), jnp.where(lane == 127, 0.0, up[1])]
        for h in range(2):
            total = below[h] + above[h]
            total = total + field[h, pl.ds(pl.multiple_of(first - CY, 8), CY), :]
            total = total + field[h, pl.ds(pl.multiple_of(first + CY, 8), CY), :]
            low = y_edge[0, h, pl.ds(CX * c + x, 1), :]
            high = y_edge[1, h, pl.ds(CX * c + x, 1), :]
            total = total + jnp.where(row == 0, low, field[h, pl.ds(first - 1, CY), :])
            total = total + jnp.where(row == CY - 1, high, field[h, pl.ds(first + 1, CY), :])
            rows = pl.ds(pl.multiple_of(CX * CY * c + CY * x, 8), CY)
            moved[rows, pl.ds(128 * h, 128)] = (1.0 - 6.0 * KAPPA) * cells[h] + KAPPA * total
        return carry

    lax.fori_loop(0, CX, column, 0, unroll=8)


def sum_blocks(buffer, count):
    total = buffer[0].astype(F32)
    for n in range(1, count):
        total = total + buffer[n].astype(F32)
    return total


def read_slots(slot_got):
    by = lax.axis_index("by")
    lane = iota((8, 128), 1)
    total = jnp.zeros((8, 128), F32)
    for j in range(BY):
        block = pltpu.roll(slot_got[j], lax.rem(128 + CAP * j - CAP * by, 128), 1)
        total = jnp.where(lane // CAP == j, block, total)
    return total


PAIR, PLANE, LINE, PLANE_ALL, MATE = range(5)


def step_kernel(
    corners_ref, flow_ref, learner_ref, goals_ref, embed_ref, mixer_ref, head_ref,
    moved, full, full_e, head_total, slots,
    field, turned, pieces, order, rows, embed_wide, mixer_wide, embed, mixer, mixer_t, act, slope1,
    slope2, pooled, back, second, first, rows_t, act_t, mixer_early, x_face, y_face, x_halo, y_halo, y_edge,
    head_grad, head_pair, head_got, slot_part, slot_got, own, pair_got, part, plane_got, line_got, part_e, plane_got_e,
    load_sems, weight_sems, halo_send, halo_recv, slot_sems, head_send, head_recv, job_send, job_recv,
):
    bx, by = lax.axis_index("bx"), lax.axis_index("by")
    core = lax.rem(by, 2)
    loads = load_flow(flow_ref, field, load_sems)
    weights = [
        pltpu.make_async_copy(embed_ref, embed_wide, weight_sems.at[0]),
        pltpu.make_async_copy(mixer_ref, mixer_wide, weight_sems.at[1]),
    ]
    for copy in weights:
        copy.start()
    greet()
    make_order(order)
    for block in range(3):
        for h in range(2):
            for copy in loads[block][h]:
                copy.wait()
            upright(block, h, field, turned)
    early, late = pl.ds(0, 1024), pl.ds(1024, 1024)

    def product(turned_rows, columns, along, factor):
        return jnp.dot(turned_rows[columns, along], factor[along, :], preferred_element_type=F32)

    cut(range(0, 16), corners_ref, turned, pieces)
    for copy in weights:
        copy.wait()
    order_rows(0, pieces, order, rows, rows_t)
    embed[...] = embed_wide[...].astype(BF16)
    mixer[...] = mixer_wide[...].astype(BF16)
    mixer_t[...] = mixer_wide[...].T.astype(BF16)
    fill_faces(field, x_face, y_face)
    pl.semaphore_wait(pltpu.get_barrier_semaphore(), len(partners()))
    halos = halo_copies(x_face, y_face, x_halo, y_halo, halo_send, halo_recv)
    for copy in halos:
        copy.start()
    for t in range(4):
        forward(t, rows, embed, mixer, act, act_t, slope1, slope2, pooled)
        cut(range(16 + 4 * t, 20 + 4 * t), corners_ref, turned, pieces)
    order_rows(1, pieces, order, rows, rows_t)
    head_step(0, pooled, goals_ref, learner_ref, head_ref, back, head_grad, slot_part)
    for t in range(4, 8):
        forward(t, rows, embed, mixer, act, act_t, slope1, slope2, pooled)
        second_layer_back(t - 4, back, slope2, second)
    head_step(1, pooled, goals_ref, learner_ref, head_ref, back, head_grad, slot_part)
    for half in range(2):
        part_of = pl.ds(256 * half, 256)
        mixer_early[part_of, :] = product(act_t, part_of, early, second)

    send_all("by", lambda peer: slot_part, slot_got.at[by], slot_sems.at[0], slot_sems.at[1])
    slot_got[by] = slot_part[...]
    send_mate(head_grad, head_pair, (head_send.at[0], head_recv.at[0]))

    def head_line(axis, value):
        me = where_am_i()[axis]
        block = head_got.at[axis, me]
        block[...] = value
        send_line(axis, block, (head_send.at[axis + 1], head_recv.at[axis + 1]))

    def head_line_sum(axis):
        wait_all(head_got.at[axis], head_recv.at[axis + 1])
        return sum_blocks(head_got.at[axis], 4)

    def sems(job, group):
        return job_send.at[job, group], job_recv.at[job, group]

    def start_pair(job, gradient):
        own[job] = gradient.reshape(2, 128, HID).astype(BF16)
        send_mate(own.at[job, 1 - core], pair_got.at[job], sems(job, PAIR))

    parts = (part.at[0], part.at[1], part_e)
    gots = (plane_got.at[0], plane_got.at[1], plane_got_e)
    fulls = (full.at[0, core], full.at[1, core], full_e)

    def plane_sends(job):
        me = plane_index(job)
        send_plane(job, lambda n: parts[job].at[n], gots[job].at[me], sems(job, PLANE))
        gots[job][me] = parts[job][me]

    def start_plane(job):
        wait_one(pair_got.at[job], job_recv.at[job, PAIR])
        total = (own[job, core].astype(F32) + pair_got[job].astype(F32)).astype(BF16)
        for n in range(16):
            part[job, n] = total[16 * (n // 2) : 16 * (n // 2) + 16, 256 * (n % 2) : 256 * (n % 2) + 256]
        plane_sends(job)

    def start_plane_e(gradient):
        total = gradient.astype(BF16)
        for n in range(32):
            part_e[n] = total[16 * (n // 2) : 16 * (n // 2) + 16, 256 * (n % 2) : 256 * (n % 2) + 256]
        plane_sends(2)

    def start_line(job):
        wait_all(gots[job], job_recv.at[job, PLANE])
        me = where_am_i()[LINES[job]]
        line_got[job, me] = sum_blocks(gots[job], gots[job].shape[0]).astype(BF16)
        send_line(LINES[job], line_got.at[job, me], sems(job, LINE))

    def start_plane_all(job):
        wait_all(line_got.at[job], job_recv.at[job, LINE])
        block = fulls[job].at[plane_index(job)]
        block[...] = sum_blocks(line_got.at[job], 4).astype(BF16)
        send_plane(job, lambda n: block, block, sems(job, PLANE_ALL))

    def start_mate(job):
        wait_all(fulls[job], job_recv.at[job, PLANE_ALL])
        send_mate(fulls[job], fulls[job], sems(job, MATE))

    for t in range(4, 8):
        second_layer_back(t, back, slope2, second)
    for half in range(2):
        part_of = pl.ds(256 * half, 256)
        start_pair(half, mixer_early[part_of, :] + product(act_t, part_of, late, second))
    for t in range(TILES):
        first_layer_back(t, second, mixer_t, slope1, first)
    start_plane(0)
    start_plane(1)
    start_plane_e(jnp.dot(rows_t[...], first[...], preferred_element_type=F32))

    wait_one(head_pair, head_recv.at[0])
    head_line(1, head_grad[...] + head_pair[...])
    for copy in halos:
        copy.wait()
    place_halos(x_halo, y_halo, field, y_edge)
    start_line(0)
    start_line(1)
    head_line(2, head_line_sum(1))
    diffuse(0, field, y_edge, moved)
    start_plane_all(0)
    start_plane_all(1)
    start_line(2)
    head_line(0, head_line_sum(2))
    diffuse(1, field, y_edge, moved)
    start_plane_all(2)
    wait_all(slot_got, slot_sems.at[1])
    slots[...] = read_slots(slot_got)
    diffuse(2, field, y_edge, moved)
    start_mate(0)
    start_mate(1)
    diffuse(3, field, y_edge, moved)
    head_total[...] = head_line_sum(0)
    wait_all(full_e, job_recv.at[2, PLANE_ALL])
    for job in range(2):
        wait_one(full.at[job, 1 - core], job_recv.at[job, MATE])
    wait_all(slot_got, slot_sems.at[0])
    wait_one(head_pair, head_send.at[0])
    for axis in range(3):
        wait_all(head_got.at[axis], head_send.at[axis + 1])
    for job in range(3):
        wait_all(gots[job], job_send.at[job, PLANE])
        wait_all(line_got.at[job], job_send.at[job, LINE])
        wait_all(fulls[job], job_send.at[job, PLANE_ALL])
    for job in range(2):
        wait_one(pair_got.at[job], job_send.at[job, PAIR])
        wait_one(fulls[job], job_send.at[job, MATE])


def scale_of(square_sum, count):
    return lax.rsqrt(jnp.sum(square_sum, keepdims=True) * (1.0 / count) + EPSILON)


def write_sum(blocks, wide, out, sems):
    total = jnp.zeros((16, 256), F32)
    for block in blocks:
        value = block[...].astype(F32)
        total = total + value * value
    scale = scale_of(total, len(blocks) * 16 * 256)
    copies = []
    for n, block in enumerate(blocks):
        wide[pl.ds(16 * (n // 2), 16), pl.ds(256 * (n % 2), 256)] = block[...].astype(F32) * scale
        if n % 16 == 15:
            rows = pl.ds(128 * (n // 16), 128)
            copies.append(pltpu.make_async_copy(wide.at[rows], out.at[rows], sems.at[n // 16]))
            copies[-1].start()
    return copies


def finish_kernel(
    moved, full, full_e, head_total, slots, flow_out, slot_out, embed_out, mixer_out, head_out,
    embed_wide, mixer_wide, flow_sems, embed_sems, mixer_sems,
):
    copies = []
    for n in range(8):
        part = pl.ds(COLS // 8 * n, COLS // 8)
        copies.append(pltpu.make_async_copy(moved.at[part], flow_out.at[part], flow_sems.at[n]))
    for copy in copies:
        copy.start()
    copies += write_sum(
        [full.at[j, h, n] for j in range(2) for h in range(2) for n in range(16)],
        mixer_wide, mixer_out, mixer_sems,
    )
    copies += write_sum([full_e.at[n] for n in range(32)], embed_wide, embed_out, embed_sems)
    total = head_total[...]
    total = total * scale_of(total * total, 3 * HID)
    for k in range(3):
        head_out[k : k + 1, 0:256] = total[k : k + 1]
        head_out[k : k + 1, 256:512] = total[k + 3 : k + 4]
        slot_out[k] = slots[k : k + 1, 0:64]
    for copy in copies:
        copy.wait()


SCRATCH = [
    pltpu.VMEM((2, CHAN * SLAB, 128), F32),
    pltpu.VMEM((CY * CZ + 32, 128), F32),
    pltpu.VMEM((512, 1024), BF16),
    pltpu.VMEM((1024, 1024), BF16),
    pltpu.VMEM((2048, FEAT), BF16),
    pltpu.VMEM((FEAT, HID), F32),
    pltpu.VMEM((HID, HID), F32),
    pltpu.VMEM((FEAT, HID), BF16),
    pltpu.VMEM((HID, HID), BF16),
    pltpu.VMEM((HID, HID), BF16),
    pltpu.VMEM((2048, HID), BF16),
    pltpu.VMEM((2048, HID), F32),
    pltpu.VMEM((2048, HID), F32),
    pltpu.VMEM((TILES, 4, HID), F32),
    pltpu.VMEM((TILES, 4, HID), F32),
    pltpu.VMEM((2048, HID), BF16),
    pltpu.VMEM((2048, HID), BF16),
    pltpu.VMEM((FEAT, 2048), BF16),
    pltpu.VMEM((HID, 2048), BF16),
    pltpu.VMEM((HID, HID), F32),
    pltpu.VMEM((2, 2, CHAN * CY, 128), BF16),
    pltpu.VMEM((2, 2, CHAN * CX, 128), BF16),
    pltpu.VMEM((2, 2, CHAN * CY, 128), BF16),
    pltpu.VMEM((2, 2, CHAN * CX, 128), BF16),
    pltpu.VMEM((2, 2, CHAN * CX, 128), F32),
    pltpu.VMEM((8, 256), F32),
    pltpu.VMEM((8, 256), F32),
    pltpu.VMEM((3, 4, 8, 256), F32),
    pltpu.VMEM((8, 128), F32),
    pltpu.VMEM((BY, 8, 128), F32),
    pltpu.VMEM((2, 2, 128, HID), BF16),
    pltpu.VMEM((2, 128, HID), BF16),
    pltpu.VMEM((2, 16, 16, 256), BF16),
    pltpu.VMEM((2, 16, 16, 256), BF16),
    pltpu.VMEM((3, 4, 16, 256), BF16),
    pltpu.VMEM((32, 16, 256), BF16),
    pltpu.VMEM((32, 16, 256), BF16),
    pltpu.SemaphoreType.DMA((3, 2, CHAN)),
    pltpu.SemaphoreType.DMA((2,)),
    pltpu.SemaphoreType.DMA((4,)),
    pltpu.SemaphoreType.DMA((4,)),
    pltpu.SemaphoreType.DMA((2,)),
    pltpu.SemaphoreType.DMA((4,)),
    pltpu.SemaphoreType.DMA((4,)),
    pltpu.SemaphoreType.DMA((3, 5)),
    pltpu.SemaphoreType.DMA((3, 5)),
]


def per_device(
    flow_field, patch_corners, patch_learner, drag_target, embed_weight, mixer_weight, head_weight
):
    vmem = pl.BlockSpec(memory_space=pltpu.VMEM)
    anywhere = pl.BlockSpec(memory_space=pl.ANY)
    parts = pl.pallas_call(
        step_kernel,
        out_shape=(
            pltpu.VMEM((COLS, CZ), F32),
            pltpu.VMEM((2, 2, 16, 16, 256), BF16),
            pltpu.VMEM((32, 16, 256), BF16),
            pltpu.VMEM((8, 256), F32),
            pltpu.VMEM((8, 128), F32),
        ),
        in_specs=[pl.BlockSpec(memory_space=pltpu.SMEM), anywhere, vmem, vmem, anywhere, anywhere, vmem],
        out_specs=(vmem,) * 5,
        scratch_shapes=SCRATCH,
        compiler_params=pltpu.CompilerParams(
            collective_id=0, has_side_effects=True, vmem_limit_bytes=44 * 2**20
        ),
    )(
        *(
            pltpu.with_memory_space_constraint(value, pltpu.HBM)
            for value in (
                patch_corners, flow_field.reshape(CHAN * CX, CY, CZ), patch_learner.reshape(1, PB),
                drag_target.reshape(3, PB), embed_weight, mixer_weight, head_weight,
            )
        )
    )
    flow, slots, embed, mixer, head = pl.pallas_call(
        finish_kernel,
        out_shape=(
            jax.ShapeDtypeStruct((COLS, CZ), F32),
            jax.ShapeDtypeStruct((3, 1, 64), F32),
            jax.ShapeDtypeStruct((FEAT, HID), F32),
            jax.ShapeDtypeStruct((HID, HID), F32),
            jax.ShapeDtypeStruct((3, HID), F32),
        ),
        in_specs=[vmem] * 5,
        out_specs=(anywhere, vmem, anywhere, anywhere, vmem),
        scratch_shapes=[
            pltpu.VMEM((FEAT, HID), F32),
            pltpu.VMEM((HID, HID), F32),
            pltpu.SemaphoreType.DMA((8,)),
            pltpu.SemaphoreType.DMA((2,)),
            pltpu.SemaphoreType.DMA((4,)),
        ],
        compiler_params=pltpu.CompilerParams(vmem_limit_bytes=16 * 2**20),
    )(*parts)
    return flow.reshape(CHAN, CX, CY, CZ), slots, embed, mixer, head


def solution(mesh):
    return jax.shard_map(
        per_device,
        mesh=mesh,
        in_specs=(
            P(None, "bx", "by", None),
            P(None, "bx", "by"),
            P("bx", "by", None),
            P(None, "bx", "by"),
            P(),
            P(),
            P(),
        ),
        out_specs=(P(None, "bx", "by", None), P(None, "bx", "by"), P(), P(), P()),
        check_vma=False,
    )
```

```python
import functools
import jax
import jax.numpy as jnp
from jax import lax
from jax.experimental import pallas as pl
from jax.experimental.pallas import tpu as pltpu
from jax.sharding import PartitionSpec as P

CHAN, CX, CY, CZ = 4, 32, 24, 256
PB, CAP, HID, FEAT = 32, 4, 512, 256
COLS = CHAN * CX * CY
SLAB = (CX + 2) * CY
BX, BY = 8, 16
MESH = pl.DeviceIdType.MESH
TILES = 8
KAPPA = 0.15
EPSILON = 1e-06
GELU_S = 0.7978845608028654
GELU_C = 0.044715
F32, BF16 = jnp.float32, jnp.bfloat16


def iota(shape, axis):
    return lax.broadcasted_iota(jnp.int32, shape, axis)


def gelu_and_slope(x):
    x2 = x * x
    t = jnp.tanh(x * (x2 * (GELU_S * GELU_C) + GELU_S))
    h = 0.5 * t + 0.5
    value = x * h
    return value, h + value * (1.0 - h) * (x2 * (6.0 * GELU_S * GELU_C) + 2.0 * GELU_S)


def load_flow(flow_ref, field, sems):
    cells = field.reshape(2, CHAN * (CX + 2), CY, 128)

    def copy(block, h, c):
        levels = pl.ds(8 * block, 8)
        return pltpu.make_async_copy(
            flow_ref.at[pl.ds(CX * c, CX), levels, pl.ds(128 * h, 128)],
            cells.at[h, pl.ds((CX + 2) * c + 1, CX), levels],
            sems.at[block, h, c],
        )

    copies = [[[copy(block, h, c) for c in range(CHAN)] for h in range(2)] for block in range(3)]
    for copy in sum(sum(copies, []), []):
        copy.start()
    return copies


def level_of(field, h, y):
    return jnp.concatenate(
        [field[h, pl.ds(SLAB * c + CY + y, CX, stride=CY), :] for c in range(CHAN)], 0
    )


def upright(block, h, field, turned):
    for y in range(8 * block, 8 * block + 8):
        turned[pl.ds(y * CZ + 128 * h, 128), :] = level_of(field, h, y).T


def cut(patches, corners_ref, turned, pieces):
    upper = iota((8, 128), 0) < 4
    even = iota((8, 128), 1) % 32 < 16
    for p in patches:
        x0, y0, z0 = corners_ref[0, 0, p], corners_ref[1, 0, p], corners_ref[2, 0, p]
        base = y0 * CZ + z0
        back = lax.rem(128 - x0, 128)
        for pair in range(8):
            halves = []
            for cy in (0, 2):
                both = []
                for parity in range(2):
                    fy, fz = divmod(2 * pair + parity, 4)
                    first = base + (4 * cy + fy) * CZ + fz
                    a = turned[pl.ds(first, 8, stride=4), :]
                    b = turned[pl.ds(first + 4 * CZ - 16, 8, stride=4), :]
                    both.append(
                        pltpu.roll(jnp.where(upper, a, b), back + 16 * parity, 1)
                    )
                halves.append(jnp.where(even, both[0], both[1]))
            pieces[pl.ds(16 * p, 16), pl.ds(128 * pair, 128)] = jnp.concatenate(halves, 0).astype(BF16)


def make_order(order):
    for block in range(8):
        k = iota((128, 1), 0)
        c, parity, cx, fx = k // 32, k // 16 % 2, k // 4 % 4, k % 4
        fyz = 2 * block + parity
        target = cx * FEAT + c * 64 + fx * 16 + fyz
        hit = iota((128, 4 * FEAT), 1) == target
        order[pl.ds(128 * block, 128), :] = jnp.where(hit, 1.0, 0.0).astype(BF16)


def order_rows(half, pieces, order, rows, rows_t):
    tiles = range(4 * half, 4 * half + 4)
    for cx in range(4):
        got = jnp.dot(
            pieces[pl.ds(256 * half, 256), :],
            order[:, pl.ds(FEAT * cx, FEAT)],
            preferred_element_type=F32,
        ).astype(BF16)
        for n, t in enumerate(tiles):
            rows[pl.ds(256 * t + 64 * cx, 64), :] = got[64 * n : 64 * n + 64]
    for t in tiles:
        rows_t[:, pl.ds(256 * t, 256)] = rows[pl.ds(256 * t, 256), :].T


def forward(t, rows, embed, mixer, act, act_t, slope1, slope2, pooled):
    at = pl.ds(t * 256, 256)
    for n in range(2):
        columns = pl.ds(256 * n, 256)
        pre = jnp.dot(rows[at, :], embed[:, columns], preferred_element_type=F32)
        value, slope = gelu_and_slope(pre)
        value = value.astype(BF16)
        act[at, columns] = value
        act_t[columns, at] = value.T
        slope1[at, columns] = slope
    for n in range(2):
        columns = pl.ds(256 * n, 256)
        pre = jnp.dot(act[at, :], mixer[:, columns], preferred_element_type=F32)
        value, slope = gelu_and_slope(pre)
        slope2[at, columns] = slope
        value = value.reshape(4, 4, 16, 256).sum(axis=0).sum(axis=1)
        pooled[t, :, columns] = value * (1.0 / 64)


def head_step(half, pooled_ref, goals_ref, learner_ref, head_ref, back, head_grad, slot_part):
    some = PB // 2
    first = some * half
    pooled = pooled_ref[pl.ds(4 * half, 4)].reshape(some, HID)
    head = head_ref[...]
    patch = iota((some, PB), 0) + first
    other = iota((some, PB), 1)
    learner_row = learner_ref[...]
    learner = jnp.sum(jnp.where(patch == other, learner_row, 0), axis=1, keepdims=True)
    earlier = (learner == learner_row) & (other < patch)
    within = jnp.sum(jnp.where(earlier, 1, 0), axis=1, keepdims=True)
    slot = learner * CAP + within
    place = iota((some, 128), 1) == slot
    total = jnp.zeros((some, HID), F32)
    head_rows, slot_rows = [], []
    for k in range(3):
        weight = head[k : k + 1, :]
        predicted = jnp.sum(pooled * weight, axis=1, keepdims=True)
        goal = goals_ref[k : k + 1, :].astype(F32)
        goal = jnp.sum(jnp.where(patch == other, goal, 0.0), axis=1, keepdims=True)
        misfit = 2.0 * (predicted - goal)
        total = total + misfit * weight
        head_rows.append(jnp.sum(misfit * pooled, axis=0, keepdims=True))
        slot_rows.append(jnp.sum(jnp.where(place, predicted, 0.0), axis=0, keepdims=True))
    back[pl.ds(4 * half, 4)] = (total * (1.0 / 64)).reshape(4, 4, HID)
    if half == 0:
        head_grad[...] = jnp.zeros_like(head_grad)
        slot_part[...] = jnp.zeros_like(slot_part)
    for k in range(3):
        head_grad[k : k + 1, :] += head_rows[k][:, 0:256]
        head_grad[k + 3 : k + 4, :] += head_rows[k][:, 256:512]
        slot_part[k : k + 1, :] += slot_rows[k]


def second_layer_back(t, back, slope2, second):
    at = pl.ds(t * 256, 256)
    for n in range(2):
        columns = pl.ds(256 * n, 256)
        slope = slope2[at, columns].reshape(4, 4, 16, 256)
        value = slope * back[t, :, columns][None, :, None, :]
        second[at, columns] = value.reshape(256, 256).astype(BF16)


def first_layer_back(t, second, mixer_t, slope1, first):
    at = pl.ds(t * 256, 256)
    for n in range(2):
        columns = pl.ds(256 * n, 256)
        value = jnp.dot(second[at, :], mixer_t[:, columns], preferred_element_type=F32)
        first[at, columns] = (value * slope1[at, columns]).astype(BF16)


def send_all(axis, source, target, send_sem, recv_sem):
    bx, by = lax.axis_index("bx"), lax.axis_index("by")
    me, size = (by, BY) if axis == "by" else (bx, BX)

    def step(distance, carry):
        peer = lax.rem(me + distance, size)
        pltpu.make_async_remote_copy(
            src_ref=source(peer),
            dst_ref=target,
            send_sem=send_sem,
            recv_sem=recv_sem,
            device_id=(bx, peer) if axis == "by" else (peer, by),
            device_id_type=MESH,
        ).start()
        return carry

    lax.fori_loop(1, size, step, 0)


def wait_all(buffer, sem):
    blocks = buffer.at[pl.ds(0, buffer.shape[0] - 1)]
    pltpu.make_async_copy(blocks, blocks, sem).wait()


def where_am_i():
    bx, by = lax.axis_index("bx"), lax.axis_index("by")
    div, rem = lax.div, lax.rem
    return [div(bx, 2), rem(div(by, 2), 4), div(by, 8) * 2 + rem(bx, 2), rem(by, 2)]


def device_at(place):
    x, y, z, core = place
    return (x * 2 + lax.rem(z, 2), lax.div(z, 2) * 8 + y * 2 + core)


PLANES = ((0, 1), (1, 2), (2, 0))
LINES = (2, 0, 1)


def plane_peers(job):
    place = where_am_i()
    first, second = PLANES[job]
    turns = [[lax.rem(place[axis] + d, 4) for d in range(4)] for axis in (first, second)]
    peers = []
    for d in (10, 6, 14, 9, 11, 2, 8, 5, 7, 13, 15, 1, 3, 4, 12, 0):
        for other in (0, 1) if job == 2 else (0,):
            if d == 0 and other == 0:
                continue
            there = list(place)
            there[first], there[second] = turns[0][d // 4], turns[1][d % 4]
            block = there[first] * 4 + there[second]
            if other:
                there[3] = 1 - place[3]
            if job == 2:
                block = block + 16 * there[3]
            peers.append((block, device_at(there)))
    return peers


def plane_index(job):
    place = where_am_i()
    first, second = PLANES[job]
    block = place[first] * 4 + place[second]
    return block + 16 * place[3] if job == 2 else block


def mate():
    place = where_am_i()
    place[3] = 1 - place[3]
    return device_at(place)


def partners():
    found = set()
    for y in range(4):
        for z in (0, 2):
            found.update((0, y, z, core) for core in (0, 1))
    for job in range(3):
        for d in range(16):
            there = [0, 0, 0, 0]
            there[PLANES[job][0]], there[PLANES[job][1]] = d // 4, d % 4
            for core in (0, 1) if job == 2 else (0,):
                there[3] = core
                found.add(tuple(there))
    return sorted(found - {(0, 0, 0, 0)})


def greet():
    barrier = pltpu.get_barrier_semaphore()
    here = where_am_i()
    turns = [[lax.rem(here[axis] + d, 4) for d in range(4)] for axis in range(3)]
    for x, y, z, core in partners():
        device = device_at((turns[0][x], turns[1][y], turns[2][z], 1 - here[3] if core else here[3]))
        pl.semaphore_signal(barrier, inc=1, device_id=device, device_id_type=MESH)


def send_plane(job, source, target, sems):
    for n, device in plane_peers(job):
        pltpu.make_async_remote_copy(
            src_ref=source(n),
            dst_ref=target,
            send_sem=sems[0],
            recv_sem=sems[1],
            device_id=device,
            device_id_type=MESH,
        ).start()


def send_line(axis, block, sems):
    for distance in (2, 1, 3):
        place = where_am_i()
        place[axis] = lax.rem(place[axis] + distance, 4)
        pltpu.make_async_remote_copy(
            src_ref=block,
            dst_ref=block,
            send_sem=sems[0],
            recv_sem=sems[1],
            device_id=device_at(place),
            device_id_type=MESH,
        ).start()


def send_mate(source, target, sems):
    pltpu.make_async_remote_copy(
        src_ref=source,
        dst_ref=target,
        send_sem=sems[0],
        recv_sem=sems[1],
        device_id=mate(),
        device_id_type=MESH,
    ).start()


def wait_one(buffer, sem):
    pltpu.make_async_copy(buffer, buffer, sem).wait()


def fill_faces(field, x_face, y_face):
    for h in range(2):
        for side, x in ((0, 0), (1, CX - 1)):
            layers = [field[h, pl.ds(SLAB * c + CY * (x + 1), CY), :] for c in range(CHAN)]
            x_face[side, h] = jnp.concatenate(layers, 0).astype(BF16)
        for side, y in ((0, 0), (1, CY - 1)):
            y_face[side, h] = level_of(field, h, y).astype(BF16)


def halo_copies(x_face, y_face, x_halo, y_halo, send_sems, recv_sems):
    bx, by = lax.axis_index("bx"), lax.axis_index("by")
    copies = []
    for n, (face, halo, device) in enumerate(
        (
            (x_face.at[1], x_halo.at[0], (lax.rem(bx + 1, BX), by)),
            (x_face.at[0], x_halo.at[1], (lax.rem(bx + BX - 1, BX), by)),
            (y_face.at[1], y_halo.at[0], (bx, lax.rem(by + 1, BY))),
            (y_face.at[0], y_halo.at[1], (bx, lax.rem(by + BY - 1, BY))),
        )
    ):
        copies.append(
            pltpu.make_async_remote_copy(
                src_ref=face,
                dst_ref=halo,
                send_sem=send_sems.at[n],
                recv_sem=recv_sems.at[n],
                device_id=device,
                device_id_type=MESH,
            )
        )
    return copies


def place_halos(x_halo, y_halo, field, y_edge):
    for h in range(2):
        for side, slot in ((0, 0), (1, CX + 1)):
            layers = x_halo[side, h].astype(F32)
            for c in range(CHAN):
                rows = pl.ds(SLAB * c + CY * slot, CY)
                field[h, rows, :] = layers[CY * c : CY * c + CY]
            y_edge[side, h] = y_halo[side, h].astype(F32)


def diffuse(c, field, y_edge, moved):
    row, lane = iota((CY, 128), 0), iota((CY, 128), 1)

    def column(x, carry):
        first = SLAB * c + CY + CY * x
        here = pl.ds(pl.multiple_of(first, 8), CY)
        cells = [field[h, here, :] for h in range(2)]
        down = [pltpu.roll(cells[h], 1, 1) for h in range(2)]
        up = [pltpu.roll(cells[h], 127, 1) for h in range(2)]
        below = [jnp.where(lane == 0, 0.0, down[0]), jnp.where(lane == 0, down[0], down[1])]
        above = [jnp.where(lane == 127, up[1], up[0]), jnp.where(lane == 127, 0.0, up[1])]
        for h in range(2):
            total = below[h] + above[h]
            total = total + field[h, pl.ds(pl.multiple_of(first - CY, 8), CY), :]
            total = total + field[h, pl.ds(pl.multiple_of(first + CY, 8), CY), :]
            low = y_edge[0, h, pl.ds(CX * c + x, 1), :]
            high = y_edge[1, h, pl.ds(CX * c + x, 1), :]
            total = total + jnp.where(row == 0, low, field[h, pl.ds(first - 1, CY), :])
            total = total + jnp.where(row == CY - 1, high, field[h, pl.ds(first + 1, CY), :])
            rows = pl.ds(pl.multiple_of(CX * CY * c + CY * x, 8), CY)
            moved[rows, pl.ds(128 * h, 128)] = (1.0 - 6.0 * KAPPA) * cells[h] + KAPPA * total
        return carry

    lax.fori_loop(0, CX, column, 0, unroll=8)


def sum_blocks(buffer, count):
    total = buffer[0].astype(F32)
    for n in range(1, count):
        total = total + buffer[n].astype(F32)
    return total


def read_slots(slot_got):
    by = lax.axis_index("by")
    lane = iota((8, 128), 1)
    total = jnp.zeros((8, 128), F32)
    for j in range(BY):
        block = pltpu.roll(slot_got[j], lax.rem(128 + CAP * j - CAP * by, 128), 1)
        total = jnp.where(lane // CAP == j, block, total)
    return total


PAIR, PLANE, LINE, PLANE_ALL, MATE = range(5)


def step_kernel(
    corners_in, flow_ref, learner_in, goals_in, embed_ref, mixer_ref, head_in,
    moved, full, full_e, head_total, slots,
    corners_ref, learner_ref, goals_ref, head_ref, field, turned, pieces, order, rows, embed_wide, mixer_wide, embed, mixer, mixer_t, act, slope1,
    slope2, pooled, back, second, first, rows_t, act_t, mixer_early, x_face, y_face, x_halo, y_halo, y_edge,
    head_grad, head_pair, head_got, slot_part, slot_got, own, pair_got, part, plane_got, line_got, part_e, plane_got_e,
    load_sems, weight_sems, halo_send, halo_recv, slot_sems, head_send, head_recv, job_send, job_recv,
):
    bx, by = lax.axis_index("bx"), lax.axis_index("by")
    core = lax.rem(by, 2)
    loads = load_flow(flow_ref, field, load_sems)
    corners = pltpu.make_async_copy(corners_in, corners_ref, weight_sems.at[0])
    corners.start()
    weights = [
        pltpu.make_async_copy(source, target, weight_sems.at[n + 1])
        for n, (source, target) in enumerate(
            (
                (embed_ref, embed_wide), (mixer_ref, mixer_wide), (learner_in, learner_ref),
                (goals_in, goals_ref), (head_in, head_ref),
            )
        )
    ]
    for copy in weights:
        copy.start()
    greet()
    make_order(order)
    for block in range(3):
        for h in range(2):
            for copy in loads[block][h]:
                copy.wait()
            upright(block, h, field, turned)
    early, late = pl.ds(0, 1024), pl.ds(1024, 1024)

    def product(turned_rows, columns, along, factor):
        return jnp.dot(turned_rows[columns, along], factor[along, :], preferred_element_type=F32)

    corners.wait()
    cut(range(0, 16), corners_ref, turned, pieces)
    for copy in weights:
        copy.wait()
    order_rows(0, pieces, order, rows, rows_t)
    embed[...] = embed_wide[...].astype(BF16)
    mixer[...] = mixer_wide[...].astype(BF16)
    mixer_t[...] = mixer_wide[...].T.astype(BF16)
    fill_faces(field, x_face, y_face)
    pl.semaphore_wait(pltpu.get_barrier_semaphore(), len(partners()))
    halos = halo_copies(x_face, y_face, x_halo, y_halo, halo_send, halo_recv)
    for copy in halos:
        copy.start()
    for t in range(4):
        forward(t, rows, embed, mixer, act, act_t, slope1, slope2, pooled)
        cut(range(16 + 4 * t, 20 + 4 * t), corners_ref, turned, pieces)
    order_rows(1, pieces, order, rows, rows_t)
    head_step(0, pooled, goals_ref, learner_ref, head_ref, back, head_grad, slot_part)
    for t in range(4, 8):
        forward(t, rows, embed, mixer, act, act_t, slope1, slope2, pooled)
        second_layer_back(t - 4, back, slope2, second)
    head_step(1, pooled, goals_ref, learner_ref, head_ref, back, head_grad, slot_part)
    for half in range(2):
        part_of = pl.ds(256 * half, 256)
        mixer_early[part_of, :] = product(act_t, part_of, early, second)

    send_all("by", lambda peer: slot_part, slot_got.at[by], slot_sems.at[0], slot_sems.at[1])
    slot_got[by] = slot_part[...]
    send_mate(head_grad, head_pair, (head_send.at[0], head_recv.at[0]))

    def head_line(axis, value):
        me = where_am_i()[axis]
        block = head_got.at[axis, me]
        block[...] = value
        send_line(axis, block, (head_send.at[axis + 1], head_recv.at[axis + 1]))

    def head_line_sum(axis):
        wait_all(head_got.at[axis], head_recv.at[axis + 1])
        return sum_blocks(head_got.at[axis], 4)

    def sems(job, group):
        return job_send.at[job, group], job_recv.at[job, group]

    def start_pair(job, gradient):
        own[job] = gradient.reshape(2, 128, HID).astype(BF16)
        send_mate(own.at[job, 1 - core], pair_got.at[job], sems(job, PAIR))

    parts = (part.at[0], part.at[1], part_e)
    gots = (plane_got.at[0], plane_got.at[1], plane_got_e)
    fulls = (full.at[0, core], full.at[1, core], full_e)

    def plane_sends(job):
        me = plane_index(job)
        send_plane(job, lambda n: parts[job].at[n], gots[job].at[me], sems(job, PLANE))
        gots[job][me] = parts[job][me]

    def start_plane(job):
        wait_one(pair_got.at[job], job_recv.at[job, PAIR])
        total = (own[job, core].astype(F32) + pair_got[job].astype(F32)).astype(BF16)
        for n in range(16):
            part[job, n] = total[16 * (n // 2) : 16 * (n // 2) + 16, 256 * (n % 2) : 256 * (n % 2) + 256]
        plane_sends(job)

    def start_plane_e(gradient):
        total = gradient.astype(BF16)
        for n in range(32):
            part_e[n] = total[16 * (n // 2) : 16 * (n // 2) + 16, 256 * (n % 2) : 256 * (n % 2) + 256]
        plane_sends(2)

    def start_line(job):
        wait_all(gots[job], job_recv.at[job, PLANE])
        me = where_am_i()[LINES[job]]
        line_got[job, me] = sum_blocks(gots[job], gots[job].shape[0]).astype(BF16)
        send_line(LINES[job], line_got.at[job, me], sems(job, LINE))

    def start_plane_all(job):
        wait_all(line_got.at[job], job_recv.at[job, LINE])
        block = fulls[job].at[plane_index(job)]
        block[...] = sum_blocks(line_got.at[job], 4).astype(BF16)
        send_plane(job, lambda n: block, block, sems(job, PLANE_ALL))

    def start_mate(job):
        wait_all(fulls[job], job_recv.at[job, PLANE_ALL])
        send_mate(fulls[job], fulls[job], sems(job, MATE))

    for t in range(4, 8):
        second_layer_back(t, back, slope2, second)
    for half in range(2):
        part_of = pl.ds(256 * half, 256)
        start_pair(half, mixer_early[part_of, :] + product(act_t, part_of, late, second))
    for t in range(TILES):
        first_layer_back(t, second, mixer_t, slope1, first)
    start_plane(0)
    start_plane(1)
    start_plane_e(jnp.dot(rows_t[...], first[...], preferred_element_type=F32))

    wait_one(head_pair, head_recv.at[0])
    head_line(1, head_grad[...] + head_pair[...])
    for copy in halos:
        copy.wait()
    place_halos(x_halo, y_halo, field, y_edge)
    start_line(0)
    start_line(1)
    head_line(2, head_line_sum(1))
    diffuse(0, field, y_edge, moved)
    start_plane_all(0)
    start_plane_all(1)
    start_line(2)
    head_line(0, head_line_sum(2))
    diffuse(1, field, y_edge, moved)
    start_plane_all(2)
    wait_all(slot_got, slot_sems.at[1])
    slots[...] = read_slots(slot_got)
    diffuse(2, field, y_edge, moved)
    start_mate(0)
    start_mate(1)
    diffuse(3, field, y_edge, moved)
    head_total[...] = head_line_sum(0)
    wait_all(full_e, job_recv.at[2, PLANE_ALL])
    for job in range(2):
        wait_one(full.at[job, 1 - core], job_recv.at[job, MATE])
    wait_all(slot_got, slot_sems.at[0])
    wait_one(head_pair, head_send.at[0])
    for axis in range(3):
        wait_all(head_got.at[axis], head_send.at[axis + 1])
    for job in range(3):
        wait_all(gots[job], job_send.at[job, PLANE])
        wait_all(line_got.at[job], job_send.at[job, LINE])
        wait_all(fulls[job], job_send.at[job, PLANE_ALL])
    for job in range(2):
        wait_one(pair_got.at[job], job_send.at[job, PAIR])
        wait_one(fulls[job], job_send.at[job, MATE])


def scale_of(square_sum, count):
    return lax.rsqrt(jnp.sum(square_sum, keepdims=True) * (1.0 / count) + EPSILON)


def write_sum(blocks, wide, out, sems):
    total = jnp.zeros((16, 256), F32)
    for block in blocks:
        value = block[...].astype(F32)
        total = total + value * value
    scale = scale_of(total, len(blocks) * 16 * 256)
    copies = []
    for n, block in enumerate(blocks):
        wide[pl.ds(16 * (n // 2), 16), pl.ds(256 * (n % 2), 256)] = block[...].astype(F32) * scale
        if n % 16 == 15:
            rows = pl.ds(128 * (n // 16), 128)
            copies.append(pltpu.make_async_copy(wide.at[rows], out.at[rows], sems.at[n // 16]))
            copies[-1].start()
    return copies


def finish_kernel(
    moved, full, full_e, head_total, slots, flow_out, slot_out, embed_out, mixer_out, head_out,
    slot_wide, head_wide, embed_wide, mixer_wide, flow_sems, small_sems, embed_sems, mixer_sems,
):
    copies = []
    for n in range(8):
        part = pl.ds(COLS // 8 * n, COLS // 8)
        copies.append(pltpu.make_async_copy(moved.at[part], flow_out.at[part], flow_sems.at[n]))
    for copy in copies:
        copy.start()
    total = head_total[...]
    total = total * scale_of(total * total, 3 * HID)
    for k in range(3):
        head_wide[k : k + 1, 0:256] = total[k : k + 1]
        head_wide[k : k + 1, 256:512] = total[k + 3 : k + 4]
        slot_wide[k] = slots[k : k + 1, 0:64]
    for n, (source, target) in enumerate(((slot_wide, slot_out), (head_wide, head_out))):
        copies.append(pltpu.make_async_copy(source, target, small_sems.at[n]))
        copies[-1].start()
    copies += write_sum(
        [full.at[j, h, n] for j in range(2) for h in range(2) for n in range(16)],
        mixer_wide, mixer_out, mixer_sems,
    )
    copies += write_sum([full_e.at[n] for n in range(32)], embed_wide, embed_out, embed_sems)
    for copy in copies:
        copy.wait()


SCRATCH = [
    pltpu.SMEM((3, 1, PB), jnp.int32),
    pltpu.VMEM((1, PB), jnp.int32),
    pltpu.VMEM((3, PB), BF16),
    pltpu.VMEM((3, HID), F32),
    pltpu.VMEM((2, CHAN * SLAB, 128), F32),
    pltpu.VMEM((CY * CZ + 32, 128), F32),
    pltpu.VMEM((512, 1024), BF16),
    pltpu.VMEM((1024, 1024), BF16),
    pltpu.VMEM((2048, FEAT), BF16),
    pltpu.VMEM((FEAT, HID), F32),
    pltpu.VMEM((HID, HID), F32),
    pltpu.VMEM((FEAT, HID), BF16),
    pltpu.VMEM((HID, HID), BF16),
    pltpu.VMEM((HID, HID), BF16),
    pltpu.VMEM((2048, HID), BF16),
    pltpu.VMEM((2048, HID), F32),
    pltpu.VMEM((2048, HID), F32),
    pltpu.VMEM((TILES, 4, HID), F32),
    pltpu.VMEM((TILES, 4, HID), F32),
    pltpu.VMEM((2048, HID), BF16),
    pltpu.VMEM((2048, HID), BF16),
    pltpu.VMEM((FEAT, 2048), BF16),
    pltpu.VMEM((HID, 2048), BF16),
    pltpu.VMEM((HID, HID), F32),
    pltpu.VMEM((2, 2, CHAN * CY, 128), BF16),
    pltpu.VMEM((2, 2, CHAN * CX, 128), BF16),
    pltpu.VMEM((2, 2, CHAN * CY, 128), BF16),
    pltpu.VMEM((2, 2, CHAN * CX, 128), BF16),
    pltpu.VMEM((2, 2, CHAN * CX, 128), F32),
    pltpu.VMEM((8, 256), F32),
    pltpu.VMEM((8, 256), F32),
    pltpu.VMEM((3, 4, 8, 256), F32),
    pltpu.VMEM((8, 128), F32),
    pltpu.VMEM((BY, 8, 128), F32),
    pltpu.VMEM((2, 2, 128, HID), BF16),
    pltpu.VMEM((2, 128, HID), BF16),
    pltpu.VMEM((2, 16, 16, 256), BF16),
    pltpu.VMEM((2, 16, 16, 256), BF16),
    pltpu.VMEM((3, 4, 16, 256), BF16),
    pltpu.VMEM((32, 16, 256), BF16),
    pltpu.VMEM((32, 16, 256), BF16),
    pltpu.SemaphoreType.DMA((3, 2, CHAN)),
    pltpu.SemaphoreType.DMA((6,)),
    pltpu.SemaphoreType.DMA((4,)),
    pltpu.SemaphoreType.DMA((4,)),
    pltpu.SemaphoreType.DMA((2,)),
    pltpu.SemaphoreType.DMA((4,)),
    pltpu.SemaphoreType.DMA((4,)),
    pltpu.SemaphoreType.DMA((3, 5)),
    pltpu.SemaphoreType.DMA((3, 5)),
]


def per_device(
    flow_field, patch_corners, patch_learner, drag_target, embed_weight, mixer_weight, head_weight
):
    vmem = pl.BlockSpec(memory_space=pltpu.VMEM)
    anywhere = pl.BlockSpec(memory_space=pl.ANY)
    parts = pl.pallas_call(
        step_kernel,
        out_shape=(
            pltpu.VMEM((COLS, CZ), F32),
            pltpu.VMEM((2, 2, 16, 16, 256), BF16),
            pltpu.VMEM((32, 16, 256), BF16),
            pltpu.VMEM((8, 256), F32),
            pltpu.VMEM((8, 128), F32),
        ),
        in_specs=[anywhere] * 7,
        out_specs=(vmem,) * 5,
        scratch_shapes=SCRATCH,
        compiler_params=pltpu.CompilerParams(
            collective_id=0, has_side_effects=True, vmem_limit_bytes=44 * 2**20
        ),
    )(
        *(
            pltpu.with_memory_space_constraint(value, pltpu.HBM)
            for value in (
                patch_corners, flow_field.reshape(CHAN * CX, CY, CZ), patch_learner.reshape(1, PB),
                drag_target.reshape(3, PB), embed_weight, mixer_weight, head_weight,
            )
        )
    )
    flow, slots, embed, mixer, head = pl.pallas_call(
        finish_kernel,
        out_shape=(
            jax.ShapeDtypeStruct((COLS, CZ), F32),
            jax.ShapeDtypeStruct((3, 1, 64), F32),
            jax.ShapeDtypeStruct((FEAT, HID), F32),
            jax.ShapeDtypeStruct((HID, HID), F32),
            jax.ShapeDtypeStruct((3, HID), F32),
        ),
        in_specs=[vmem] * 5,
        out_specs=(anywhere,) * 5,
        scratch_shapes=[
            pltpu.VMEM((3, 1, 64), F32),
            pltpu.VMEM((3, HID), F32),
            pltpu.VMEM((FEAT, HID), F32),
            pltpu.VMEM((HID, HID), F32),
            pltpu.SemaphoreType.DMA((8,)),
            pltpu.SemaphoreType.DMA((2,)),
            pltpu.SemaphoreType.DMA((2,)),
            pltpu.SemaphoreType.DMA((4,)),
        ],
        compiler_params=pltpu.CompilerParams(vmem_limit_bytes=16 * 2**20),
    )(*parts)
    return flow.reshape(CHAN, CX, CY, CZ), slots, embed, mixer, head


def solution(mesh):
    return jax.shard_map(
        per_device,
        mesh=mesh,
        in_specs=(
            P(None, "bx", "by", None),
            P(None, "bx", "by"),
            P("bx", "by", None),
            P(None, "bx", "by"),
            P(),
            P(),
            P(),
        ),
        out_specs=(P(None, "bx", "by", None), P(None, "bx", "by"), P(), P(), P()),
        check_vma=False,
    )
```

```python
import functools
import jax
import jax.numpy as jnp
from jax import lax
from jax.experimental import pallas as pl
from jax.experimental.pallas import tpu as pltpu
from jax.sharding import PartitionSpec as P

CHAN, CX, CY, CZ = 4, 32, 24, 256
PB, CAP, HID, FEAT = 32, 4, 512, 256
COLS = CHAN * CX * CY
SLAB = (CX + 2) * CY
BX, BY = 8, 16
MESH = pl.DeviceIdType.MESH
TILES = 8
EARLY = 6
KAPPA = 0.15
EPSILON = 1e-06
GELU_S = 0.7978845608028654
GELU_C = 0.044715
F32, BF16 = jnp.float32, jnp.bfloat16


def iota(shape, axis):
    return lax.broadcasted_iota(jnp.int32, shape, axis)


def gelu_and_slope(x):
    x2 = x * x
    t = jnp.tanh(x * (x2 * (GELU_S * GELU_C) + GELU_S))
    h = 0.5 * t + 0.5
    value = x * h
    return value, h + value * (1.0 - h) * (x2 * (6.0 * GELU_S * GELU_C) + 2.0 * GELU_S)


def load_flow(flow_ref, field, sems):
    cells = field.reshape(2, CHAN * (CX + 2), CY, 128)

    def copy(block, h, c):
        levels = pl.ds(8 * block, 8)
        return pltpu.make_async_copy(
            flow_ref.at[pl.ds(CX * c, CX), levels, pl.ds(128 * h, 128)],
            cells.at[h, pl.ds((CX + 2) * c + 1, CX), levels],
            sems.at[block, h, c],
        )

    copies = [[[copy(block, h, c) for c in range(CHAN)] for h in range(2)] for block in range(3)]
    for copy in sum(sum(copies, []), []):
        copy.start()
    return copies


def level_of(field, h, y):
    return jnp.concatenate(
        [field[h, pl.ds(SLAB * c + CY + y, CX, stride=CY), :] for c in range(CHAN)], 0
    )


def upright(block, h, field, turned):
    for y in range(8 * block, 8 * block + 8):
        turned[pl.ds(y * CZ + 128 * h, 128), :] = level_of(field, h, y).T


def cut(patches, corners_ref, turned, pieces):
    upper = iota((8, 128), 0) < 4
    even = iota((8, 128), 1) % 32 < 16
    for p in patches:
        x0, y0, z0 = corners_ref[0, 0, p], corners_ref[1, 0, p], corners_ref[2, 0, p]
        base = y0 * CZ + z0
        back = lax.rem(128 - x0, 128)
        for pair in range(8):
            halves = []
            for cy in (0, 2):
                both = []
                for parity in range(2):
                    fy, fz = divmod(2 * pair + parity, 4)
                    first = base + (4 * cy + fy) * CZ + fz
                    a = turned[pl.ds(first, 8, stride=4), :]
                    b = turned[pl.ds(first + 4 * CZ - 16, 8, stride=4), :]
                    both.append(
                        pltpu.roll(jnp.where(upper, a, b), back + 16 * parity, 1)
                    )
                halves.append(jnp.where(even, both[0], both[1]))
            pieces[pl.ds(16 * p, 16), pl.ds(128 * pair, 128)] = jnp.concatenate(halves, 0).astype(BF16)


def make_order(order):
    for block in range(8):
        k = iota((128, 1), 0)
        c, parity, cx, fx = k // 32, k // 16 % 2, k // 4 % 4, k % 4
        fyz = 2 * block + parity
        target = cx * FEAT + c * 64 + fx * 16 + fyz
        hit = iota((128, 4 * FEAT), 1) == target
        order[pl.ds(128 * block, 128), :] = jnp.where(hit, 1.0, 0.0).astype(BF16)


def order_rows(half, pieces, order, rows, rows_t):
    tiles = range(4 * half, 4 * half + 4)
    for cx in range(4):
        got = jnp.dot(
            pieces[pl.ds(256 * half, 256), :],
            order[:, pl.ds(FEAT * cx, FEAT)],
            preferred_element_type=F32,
        ).astype(BF16)
        for n, t in enumerate(tiles):
            rows[pl.ds(256 * t + 64 * cx, 64), :] = got[64 * n : 64 * n + 64]
    for t in tiles:
        rows_t[:, pl.ds(256 * t, 256)] = rows[pl.ds(256 * t, 256), :].T


def forward(t, rows, embed, mixer, act, act_t, slope1, slope2, pooled):
    at = pl.ds(t * 256, 256)
    for n in range(2):
        columns = pl.ds(256 * n, 256)
        pre = jnp.dot(rows[at, :], embed[:, columns], preferred_element_type=F32)
        value, slope = gelu_and_slope(pre)
        value = value.astype(BF16)
        act[at, columns] = value
        act_t[columns, at] = value.T
        slope1[at, columns] = slope
    for n in range(2):
        columns = pl.ds(256 * n, 256)
        pre = jnp.dot(act[at, :], mixer[:, columns], preferred_element_type=F32)
        value, slope = gelu_and_slope(pre)
        slope2[at, columns] = slope
        value = value.reshape(4, 4, 16, 256).sum(axis=0).sum(axis=1)
        pooled[t, :, columns] = value * (1.0 / 64)


def head_step(tiles, pooled_ref, goals_ref, learner_ref, head_ref, back, head_grad, slot_part):
    some, first = 4 * len(tiles), 4 * tiles[0]
    pooled = pooled_ref[pl.ds(tiles[0], len(tiles))].reshape(some, HID)
    head = head_ref[...]
    patch = iota((some, PB), 0) + first
    other = iota((some, PB), 1)
    learner_row = learner_ref[...]
    learner = jnp.sum(jnp.where(patch == other, learner_row, 0), axis=1, keepdims=True)
    earlier = (learner == learner_row) & (other < patch)
    within = jnp.sum(jnp.where(earlier, 1, 0), axis=1, keepdims=True)
    slot = learner * CAP + within
    place = iota((some, 128), 1) == slot
    total = jnp.zeros((some, HID), F32)
    head_rows, slot_rows = [], []
    for k in range(3):
        weight = head[k : k + 1, :]
        predicted = jnp.sum(pooled * weight, axis=1, keepdims=True)
        goal = goals_ref[k : k + 1, :].astype(F32)
        goal = jnp.sum(jnp.where(patch == other, goal, 0.0), axis=1, keepdims=True)
        misfit = 2.0 * (predicted - goal)
        total = total + misfit * weight
        head_rows.append(jnp.sum(misfit * pooled, axis=0, keepdims=True))
        slot_rows.append(jnp.sum(jnp.where(place, predicted, 0.0), axis=0, keepdims=True))
    back[pl.ds(tiles[0], len(tiles))] = (total * (1.0 / 64)).reshape(len(tiles), 4, HID)
    if first == 0:
        head_grad[...] = jnp.zeros_like(head_grad)
        slot_part[...] = jnp.zeros_like(slot_part)
    for k in range(3):
        head_grad[k : k + 1, :] += head_rows[k][:, 0:256]
        head_grad[k + 3 : k + 4, :] += head_rows[k][:, 256:512]
        slot_part[k : k + 1, :] += slot_rows[k]


def second_layer_back(t, back, slope2, second):
    at = pl.ds(t * 256, 256)
    for n in range(2):
        columns = pl.ds(256 * n, 256)
        slope = slope2[at, columns].reshape(4, 4, 16, 256)
        value = slope * back[t, :, columns][None, :, None, :]
        second[at, columns] = value.reshape(256, 256).astype(BF16)


def first_layer_back(t, second, mixer_t, slope1, first):
    at = pl.ds(t * 256, 256)
    for n in range(2):
        columns = pl.ds(256 * n, 256)
        value = jnp.dot(second[at, :], mixer_t[:, columns], preferred_element_type=F32)
        first[at, columns] = (value * slope1[at, columns]).astype(BF16)


def send_all(axis, source, target, send_sem, recv_sem):
    bx, by = lax.axis_index("bx"), lax.axis_index("by")
    me, size = (by, BY) if axis == "by" else (bx, BX)

    def step(distance, carry):
        peer = lax.rem(me + distance, size)
        pltpu.make_async_remote_copy(
            src_ref=source(peer),
            dst_ref=target,
            send_sem=send_sem,
            recv_sem=recv_sem,
            device_id=(bx, peer) if axis == "by" else (peer, by),
            device_id_type=MESH,
        ).start()
        return carry

    lax.fori_loop(1, size, step, 0)


def wait_all(buffer, sem):
    blocks = buffer.at[pl.ds(0, buffer.shape[0] - 1)]
    pltpu.make_async_copy(blocks, blocks, sem).wait()


def where_am_i():
    bx, by = lax.axis_index("bx"), lax.axis_index("by")
    div, rem = lax.div, lax.rem
    return [div(bx, 2), rem(div(by, 2), 4), div(by, 8) * 2 + rem(bx, 2), rem(by, 2)]


def device_at(place):
    x, y, z, core = place
    return (x * 2 + lax.rem(z, 2), lax.div(z, 2) * 8 + y * 2 + core)


PLANES = ((0, 1), (1, 2), (2, 0))
LINES = (2, 0, 1)


def plane_peers(job):
    place = where_am_i()
    first, second = PLANES[job]
    turns = [[lax.rem(place[axis] + d, 4) for d in range(4)] for axis in (first, second)]
    peers = []
    for d in (10, 6, 14, 9, 11, 2, 8, 5, 7, 13, 15, 1, 3, 4, 12, 0):
        for other in (0, 1) if job == 2 else (0,):
            if d == 0 and other == 0:
                continue
            there = list(place)
            there[first], there[second] = turns[0][d // 4], turns[1][d % 4]
            block = there[first] * 4 + there[second]
            if other:
                there[3] = 1 - place[3]
            if job == 2:
                block = block + 16 * there[3]
            peers.append((block, device_at(there)))
    return peers


def plane_index(job):
    place = where_am_i()
    first, second = PLANES[job]
    block = place[first] * 4 + place[second]
    return block + 16 * place[3] if job == 2 else block


def mate():
    place = where_am_i()
    place[3] = 1 - place[3]
    return device_at(place)


def partners():
    found = set()
    for y in range(4):
        for z in (0, 2):
            found.update((0, y, z, core) for core in (0, 1))
    for job in range(3):
        for d in range(16):
            there = [0, 0, 0, 0]
            there[PLANES[job][0]], there[PLANES[job][1]] = d // 4, d % 4
            for core in (0, 1) if job == 2 else (0,):
                there[3] = core
                found.add(tuple(there))
    return sorted(found - {(0, 0, 0, 0)})


def greet():
    barrier = pltpu.get_barrier_semaphore()
    here = where_am_i()
    turns = [[lax.rem(here[axis] + d, 4) for d in range(4)] for axis in range(3)]
    for x, y, z, core in partners():
        device = device_at((turns[0][x], turns[1][y], turns[2][z], 1 - here[3] if core else here[3]))
        pl.semaphore_signal(barrier, inc=1, device_id=device, device_id_type=MESH)


def send_plane(job, source, target, sems):
    for n, device in plane_peers(job):
        pltpu.make_async_remote_copy(
            src_ref=source(n),
            dst_ref=target,
            send_sem=sems[0],
            recv_sem=sems[1],
            device_id=device,
            device_id_type=MESH,
        ).start()


def send_line(axis, block, sems):
    for distance in (2, 1, 3):
        place = where_am_i()
        place[axis] = lax.rem(place[axis] + distance, 4)
        pltpu.make_async_remote_copy(
            src_ref=block,
            dst_ref=block,
            send_sem=sems[0],
            recv_sem=sems[1],
            device_id=device_at(place),
            device_id_type=MESH,
        ).start()


def send_mate(source, target, sems):
    pltpu.make_async_remote_copy(
        src_ref=source,
        dst_ref=target,
        send_sem=sems[0],
        recv_sem=sems[1],
        device_id=mate(),
        device_id_type=MESH,
    ).start()


def wait_one(buffer, sem):
    pltpu.make_async_copy(buffer, buffer, sem).wait()


def fill_faces(field, x_face, y_face):
    for h in range(2):
        for side, x in ((0, 0), (1, CX - 1)):
            layers = [field[h, pl.ds(SLAB * c + CY * (x + 1), CY), :] for c in range(CHAN)]
            x_face[side, h] = jnp.concatenate(layers, 0).astype(BF16)
        for side, y in ((0, 0), (1, CY - 1)):
            y_face[side, h] = level_of(field, h, y).astype(BF16)


def halo_copies(x_face, y_face, x_halo, y_halo, send_sems, recv_sems):
    bx, by = lax.axis_index("bx"), lax.axis_index("by")
    copies = []
    for n, (face, halo, device) in enumerate(
        (
            (x_face.at[1], x_halo.at[0], (lax.rem(bx + 1, BX), by)),
            (x_face.at[0], x_halo.at[1], (lax.rem(bx + BX - 1, BX), by)),
            (y_face.at[1], y_halo.at[0], (bx, lax.rem(by + 1, BY))),
            (y_face.at[0], y_halo.at[1], (bx, lax.rem(by + BY - 1, BY))),
        )
    ):
        copies.append(
            pltpu.make_async_remote_copy(
                src_ref=face,
                dst_ref=halo,
                send_sem=send_sems.at[n],
                recv_sem=recv_sems.at[n],
                device_id=device,
                device_id_type=MESH,
            )
        )
    return copies


def place_halos(x_halo, y_halo, field, y_edge):
    for h in range(2):
        for side, slot in ((0, 0), (1, CX + 1)):
            layers = x_halo[side, h].astype(F32)
            for c in range(CHAN):
                rows = pl.ds(SLAB * c + CY * slot, CY)
                field[h, rows, :] = layers[CY * c : CY * c + CY]
            y_edge[side, h] = y_halo[side, h].astype(F32)


def diffuse(c, field, y_edge, moved):
    row, lane = iota((CY, 128), 0), iota((CY, 128), 1)

    def column(x, carry):
        first = SLAB * c + CY + CY * x
        here = pl.ds(pl.multiple_of(first, 8), CY)
        cells = [field[h, here, :] for h in range(2)]
        down = [pltpu.roll(cells[h], 1, 1) for h in range(2)]
        up = [pltpu.roll(cells[h], 127, 1) for h in range(2)]
        below = [jnp.where(lane == 0, 0.0, down[0]), jnp.where(lane == 0, down[0], down[1])]
        above = [jnp.where(lane == 127, up[1], up[0]), jnp.where(lane == 127, 0.0, up[1])]
        for h in range(2):
            total = below[h] + above[h]
            total = total + field[h, pl.ds(pl.multiple_of(first - CY, 8), CY), :]
            total = total + field[h, pl.ds(pl.multiple_of(first + CY, 8), CY), :]
            low = y_edge[0, h, pl.ds(CX * c + x, 1), :]
            high = y_edge[1, h, pl.ds(CX * c + x, 1), :]
            total = total + jnp.where(row == 0, low, field[h, pl.ds(first - 1, CY), :])
            total = total + jnp.where(row == CY - 1, high, field[h, pl.ds(first + 1, CY), :])
            rows = pl.ds(pl.multiple_of(CX * CY * c + CY * x, 8), CY)
            moved[rows, pl.ds(128 * h, 128)] = (1.0 - 6.0 * KAPPA) * cells[h] + KAPPA * total
        return carry

    lax.fori_loop(0, CX, column, 0, unroll=8)


def sum_blocks(buffer, count):
    total = buffer[0].astype(F32)
    for n in range(1, count):
        total = total + buffer[n].astype(F32)
    return total


def read_slots(slot_got):
    by = lax.axis_index("by")
    lane = iota((8, 128), 1)
    total = jnp.zeros((8, 128), F32)
    for j in range(BY):
        block = pltpu.roll(slot_got[j], lax.rem(128 + CAP * j - CAP * by, 128), 1)
        total = jnp.where(lane // CAP == j, block, total)
    return total


PAIR, PLANE, LINE, PLANE_ALL, MATE = range(5)


def step_kernel(
    corners_in, flow_ref, learner_in, goals_in, embed_ref, mixer_ref, head_in,
    moved, full, full_e, head_total, slots,
    corners_ref, learner_ref, goals_ref, head_ref, field, turned, pieces, order, rows, embed_wide, mixer_wide, embed, mixer, mixer_t, act, slope1,
    slope2, pooled, back, second, first, rows_t, act_t, mixer_early, x_face, y_face, x_halo, y_halo, y_edge,
    head_grad, head_pair, head_got, slot_part, slot_got, own, pair_got, part, plane_got, line_got, part_e, plane_got_e,
    load_sems, weight_sems, halo_send, halo_recv, slot_sems, head_send, head_recv, job_send, job_recv,
):
    bx, by = lax.axis_index("bx"), lax.axis_index("by")
    core = lax.rem(by, 2)
    loads = load_flow(flow_ref, field, load_sems)
    corners = pltpu.make_async_copy(corners_in, corners_ref, weight_sems.at[0])
    corners.start()
    weights = [
        pltpu.make_async_copy(source, target, weight_sems.at[n + 1])
        for n, (source, target) in enumerate(
            (
                (embed_ref, embed_wide), (mixer_ref, mixer_wide), (learner_in, learner_ref),
                (goals_in, goals_ref), (head_in, head_ref),
            )
        )
    ]
    for copy in weights:
        copy.start()
    greet()
    make_order(order)
    for block in range(3):
        for h in range(2):
            for copy in loads[block][h]:
                copy.wait()
            upright(block, h, field, turned)
    early, late = pl.ds(0, 256 * EARLY), pl.ds(256 * EARLY, 256 * (TILES - EARLY))

    def product(turned_rows, columns, along, factor):
        return jnp.dot(turned_rows[columns, along], factor[along, :], preferred_element_type=F32)

    corners.wait()
    cut(range(0, 16), corners_ref, turned, pieces)
    for copy in weights:
        copy.wait()
    order_rows(0, pieces, order, rows, rows_t)
    embed[...] = embed_wide[...].astype(BF16)
    mixer[...] = mixer_wide[...].astype(BF16)
    mixer_t[...] = mixer_wide[...].T.astype(BF16)
    fill_faces(field, x_face, y_face)
    pl.semaphore_wait(pltpu.get_barrier_semaphore(), len(partners()))
    halos = halo_copies(x_face, y_face, x_halo, y_halo, halo_send, halo_recv)
    for copy in halos:
        copy.start()
    for t in range(4):
        forward(t, rows, embed, mixer, act, act_t, slope1, slope2, pooled)
        cut(range(16 + 4 * t, 20 + 4 * t), corners_ref, turned, pieces)
    order_rows(1, pieces, order, rows, rows_t)
    for t in range(4, TILES):
        forward(t, rows, embed, mixer, act, act_t, slope1, slope2, pooled)
        if t == EARLY - 1:
            head_step(range(EARLY), pooled, goals_ref, learner_ref, head_ref, back, head_grad, slot_part)
        if t >= EARLY:
            for n in range(3 * (t - EARLY), 3 * (t - EARLY) + 3):
                second_layer_back(n, back, slope2, second)
    head_step(range(EARLY, TILES), pooled, goals_ref, learner_ref, head_ref, back, head_grad, slot_part)
    for half in range(2):
        part_of = pl.ds(256 * half, 256)
        mixer_early[part_of, :] = product(act_t, part_of, early, second)

    send_mate(head_grad, head_pair, (head_send.at[0], head_recv.at[0]))

    def head_line(axis, value):
        me = where_am_i()[axis]
        block = head_got.at[axis, me]
        block[...] = value
        send_line(axis, block, (head_send.at[axis + 1], head_recv.at[axis + 1]))

    def head_line_sum(axis):
        wait_all(head_got.at[axis], head_recv.at[axis + 1])
        return sum_blocks(head_got.at[axis], 4)

    def sems(job, group):
        return job_send.at[job, group], job_recv.at[job, group]

    def start_pair(job, gradient):
        own[job] = gradient.reshape(2, 128, HID).astype(BF16)
        send_mate(own.at[job, 1 - core], pair_got.at[job], sems(job, PAIR))

    parts = (part.at[0], part.at[1], part_e)
    gots = (plane_got.at[0], plane_got.at[1], plane_got_e)
    fulls = (full.at[0, core], full.at[1, core], full_e)

    def plane_sends(job):
        me = plane_index(job)
        send_plane(job, lambda n: parts[job].at[n], gots[job].at[me], sems(job, PLANE))
        gots[job][me] = parts[job][me]

    def start_plane(job):
        wait_one(pair_got.at[job], job_recv.at[job, PAIR])
        total = (own[job, core].astype(F32) + pair_got[job].astype(F32)).astype(BF16)
        for n in range(16):
            part[job, n] = total[16 * (n // 2) : 16 * (n // 2) + 16, 256 * (n % 2) : 256 * (n % 2) + 256]
        plane_sends(job)

    def start_plane_e(gradient):
        total = gradient.astype(BF16)
        for n in range(32):
            part_e[n] = total[16 * (n // 2) : 16 * (n // 2) + 16, 256 * (n % 2) : 256 * (n % 2) + 256]
        plane_sends(2)

    def start_line(job):
        wait_all(gots[job], job_recv.at[job, PLANE])
        me = where_am_i()[LINES[job]]
        line_got[job, me] = sum_blocks(gots[job], gots[job].shape[0]).astype(BF16)
        send_line(LINES[job], line_got.at[job, me], sems(job, LINE))

    def start_plane_all(job):
        wait_all(line_got.at[job], job_recv.at[job, LINE])
        block = fulls[job].at[plane_index(job)]
        block[...] = sum_blocks(line_got.at[job], 4).astype(BF16)
        send_plane(job, lambda n: block, block, sems(job, PLANE_ALL))

    def start_mate(job):
        wait_all(fulls[job], job_recv.at[job, PLANE_ALL])
        send_mate(fulls[job], fulls[job], sems(job, MATE))

    for t in range(EARLY, TILES):
        second_layer_back(t, back, slope2, second)
    for half in range(2):
        part_of = pl.ds(256 * half, 256)
        start_pair(half, mixer_early[part_of, :] + product(act_t, part_of, late, second))
    for t in range(TILES):
        first_layer_back(t, second, mixer_t, slope1, first)
    start_plane(0)
    start_plane(1)
    start_plane_e(jnp.dot(rows_t[...], first[...], preferred_element_type=F32))

    wait_one(head_pair, head_recv.at[0])
    head_line(1, head_grad[...] + head_pair[...])
    for copy in halos:
        copy.wait()
    place_halos(x_halo, y_halo, field, y_edge)
    start_line(0)
    start_line(1)
    head_line(2, head_line_sum(1))
    send_all("by", lambda peer: slot_part, slot_got.at[by], slot_sems.at[0], slot_sems.at[1])
    slot_got[by] = slot_part[...]
    diffuse(0, field, y_edge, moved)
    start_plane_all(0)
    start_plane_all(1)
    start_line(2)
    head_line(0, head_line_sum(2))
    diffuse(1, field, y_edge, moved)
    start_plane_all(2)
    wait_all(slot_got, slot_sems.at[1])
    slots[...] = read_slots(slot_got)
    diffuse(2, field, y_edge, moved)
    start_mate(0)
    start_mate(1)
    diffuse(3, field, y_edge, moved)
    head_total[...] = head_line_sum(0)
    wait_all(full_e, job_recv.at[2, PLANE_ALL])
    for job in range(2):
        wait_one(full.at[job, 1 - core], job_recv.at[job, MATE])
    wait_all(slot_got, slot_sems.at[0])
    wait_one(head_pair, head_send.at[0])
    for axis in range(3):
        wait_all(head_got.at[axis], head_send.at[axis + 1])
    for job in range(3):
        wait_all(gots[job], job_send.at[job, PLANE])
        wait_all(line_got.at[job], job_send.at[job, LINE])
        wait_all(fulls[job], job_send.at[job, PLANE_ALL])
    for job in range(2):
        wait_one(pair_got.at[job], job_send.at[job, PAIR])
        wait_one(fulls[job], job_send.at[job, MATE])


def scale_of(square_sum, count):
    return lax.rsqrt(jnp.sum(square_sum, keepdims=True) * (1.0 / count) + EPSILON)


def write_sum(blocks, wide, out, sems):
    total = jnp.zeros((16, 256), F32)
    for block in blocks:
        value = block[...].astype(F32)
        total = total + value * value
    scale = scale_of(total, len(blocks) * 16 * 256)
    copies = []
    for n, block in enumerate(blocks):
        wide[pl.ds(16 * (n // 2), 16), pl.ds(256 * (n % 2), 256)] = block[...].astype(F32) * scale
        if n % 16 == 15:
            rows = pl.ds(128 * (n // 16), 128)
            copies.append(pltpu.make_async_copy(wide.at[rows], out.at[rows], sems.at[n // 16]))
            copies[-1].start()
    return copies


def finish_kernel(
    moved, full, full_e, head_total, slots, flow_out, slot_out, embed_out, mixer_out, head_out,
    slot_wide, head_wide, embed_wide, mixer_wide, flow_sems, small_sems, embed_sems, mixer_sems,
):
    copies = []
    for n in range(8):
        part = pl.ds(COLS // 8 * n, COLS // 8)
        copies.append(pltpu.make_async_copy(moved.at[part], flow_out.at[part], flow_sems.at[n]))
    for copy in copies:
        copy.start()
    total = head_total[...]
    total = total * scale_of(total * total, 3 * HID)
    for k in range(3):
        head_wide[k : k + 1, 0:256] = total[k : k + 1]
        head_wide[k : k + 1, 256:512] = total[k + 3 : k + 4]
        slot_wide[k] = slots[k : k + 1, 0:64]
    for n, (source, target) in enumerate(((slot_wide, slot_out), (head_wide, head_out))):
        copies.append(pltpu.make_async_copy(source, target, small_sems.at[n]))
        copies[-1].start()
    copies += write_sum(
        [full.at[j, h, n] for j in range(2) for h in range(2) for n in range(16)],
        mixer_wide, mixer_out, mixer_sems,
    )
    copies += write_sum([full_e.at[n] for n in range(32)], embed_wide, embed_out, embed_sems)
    for copy in copies:
        copy.wait()


SCRATCH = [
    pltpu.SMEM((3, 1, PB), jnp.int32),
    pltpu.VMEM((1, PB), jnp.int32),
    pltpu.VMEM((3, PB), BF16),
    pltpu.VMEM((3, HID), F32),
    pltpu.VMEM((2, CHAN * SLAB, 128), F32),
    pltpu.VMEM((CY * CZ + 32, 128), F32),
    pltpu.VMEM((512, 1024), BF16),
    pltpu.VMEM((1024, 1024), BF16),
    pltpu.VMEM((2048, FEAT), BF16),
    pltpu.VMEM((FEAT, HID), F32),
    pltpu.VMEM((HID, HID), F32),
    pltpu.VMEM((FEAT, HID), BF16),
    pltpu.VMEM((HID, HID), BF16),
    pltpu.VMEM((HID, HID), BF16),
    pltpu.VMEM((2048, HID), BF16),
    pltpu.VMEM((2048, HID), F32),
    pltpu.VMEM((2048, HID), F32),
    pltpu.VMEM((TILES, 4, HID), F32),
    pltpu.VMEM((TILES, 4, HID), F32),
    pltpu.VMEM((2048, HID), BF16),
    pltpu.VMEM((2048, HID), BF16),
    pltpu.VMEM((FEAT, 2048), BF16),
    pltpu.VMEM((HID, 2048), BF16),
    pltpu.VMEM((HID, HID), F32),
    pltpu.VMEM((2, 2, CHAN * CY, 128), BF16),
    pltpu.VMEM((2, 2, CHAN * CX, 128), BF16),
    pltpu.VMEM((2, 2, CHAN * CY, 128), BF16),
    pltpu.VMEM((2, 2, CHAN * CX, 128), BF16),
    pltpu.VMEM((2, 2, CHAN * CX, 128), F32),
    pltpu.VMEM((8, 256), F32),
    pltpu.VMEM((8, 256), F32),
    pltpu.VMEM((3, 4, 8, 256), F32),
    pltpu.VMEM((8, 128), F32),
    pltpu.VMEM((BY, 8, 128), F32),
    pltpu.VMEM((2, 2, 128, HID), BF16),
    pltpu.VMEM((2, 128, HID), BF16),
    pltpu.VMEM((2, 16, 16, 256), BF16),
    pltpu.VMEM((2, 16, 16, 256), BF16),
    pltpu.VMEM((3, 4, 16, 256), BF16),
    pltpu.VMEM((32, 16, 256), BF16),
    pltpu.VMEM((32, 16, 256), BF16),
    pltpu.SemaphoreType.DMA((3, 2, CHAN)),
    pltpu.SemaphoreType.DMA((6,)),
    pltpu.SemaphoreType.DMA((4,)),
    pltpu.SemaphoreType.DMA((4,)),
    pltpu.SemaphoreType.DMA((2,)),
    pltpu.SemaphoreType.DMA((4,)),
    pltpu.SemaphoreType.DMA((4,)),
    pltpu.SemaphoreType.DMA((3, 5)),
    pltpu.SemaphoreType.DMA((3, 5)),
]


def per_device(
    flow_field, patch_corners, patch_learner, drag_target, embed_weight, mixer_weight, head_weight
):
    vmem = pl.BlockSpec(memory_space=pltpu.VMEM)
    anywhere = pl.BlockSpec(memory_space=pl.ANY)
    parts = pl.pallas_call(
        step_kernel,
        out_shape=(
            pltpu.VMEM((COLS, CZ), F32),
            pltpu.VMEM((2, 2, 16, 16, 256), BF16),
            pltpu.VMEM((32, 16, 256), BF16),
            pltpu.VMEM((8, 256), F32),
            pltpu.VMEM((8, 128), F32),
        ),
        in_specs=[anywhere] * 7,
        out_specs=(vmem,) * 5,
        scratch_shapes=SCRATCH,
        compiler_params=pltpu.CompilerParams(
            collective_id=0, has_side_effects=True, vmem_limit_bytes=44 * 2**20
        ),
    )(
        *(
            pltpu.with_memory_space_constraint(value, pltpu.HBM)
            for value in (
                patch_corners, flow_field.reshape(CHAN * CX, CY, CZ), patch_learner.reshape(1, PB),
                drag_target.reshape(3, PB), embed_weight, mixer_weight, head_weight,
            )
        )
    )
    flow, slots, embed, mixer, head = pl.pallas_call(
        finish_kernel,
        out_shape=(
            jax.ShapeDtypeStruct((COLS, CZ), F32),
            jax.ShapeDtypeStruct((3, 1, 64), F32),
            jax.ShapeDtypeStruct((FEAT, HID), F32),
            jax.ShapeDtypeStruct((HID, HID), F32),
            jax.ShapeDtypeStruct((3, HID), F32),
        ),
        in_specs=[vmem] * 5,
        out_specs=(anywhere,) * 5,
        scratch_shapes=[
            pltpu.VMEM((3, 1, 64), F32),
            pltpu.VMEM((3, HID), F32),
            pltpu.VMEM((FEAT, HID), F32),
            pltpu.VMEM((HID, HID), F32),
            pltpu.SemaphoreType.DMA((8,)),
            pltpu.SemaphoreType.DMA((2,)),
            pltpu.SemaphoreType.DMA((2,)),
            pltpu.SemaphoreType.DMA((4,)),
        ],
        compiler_params=pltpu.CompilerParams(vmem_limit_bytes=16 * 2**20),
    )(*parts)
    return flow.reshape(CHAN, CX, CY, CZ), slots, embed, mixer, head


def solution(mesh):
    return jax.shard_map(
        per_device,
        mesh=mesh,
        in_specs=(
            P(None, "bx", "by", None),
            P(None, "bx", "by"),
            P("bx", "by", None),
            P(None, "bx", "by"),
            P(),
            P(),
            P(),
        ),
        out_specs=(P(None, "bx", "by", None), P(None, "bx", "by"), P(), P(), P()),
        check_vma=False,
    )
```

```python
import functools
import jax
import jax.numpy as jnp
from jax import lax
from jax.experimental import pallas as pl
from jax.experimental.pallas import tpu as pltpu
from jax.sharding import PartitionSpec as P

CHAN, CX, CY, CZ = 4, 32, 24, 256
PB, CAP, HID, FEAT = 32, 4, 512, 256
COLS = CHAN * CX * CY
SLAB = (CX + 2) * CY
BX, BY = 8, 16
MESH = pl.DeviceIdType.MESH
TILES = 8
EARLY = 6
KAPPA = 0.15
EPSILON = 1e-06
GELU_S = 0.7978845608028654
GELU_C = 0.044715
F32, BF16 = jnp.float32, jnp.bfloat16


def iota(shape, axis):
    return lax.broadcasted_iota(jnp.int32, shape, axis)


def gelu_and_slope(x):
    x2 = x * x
    t = jnp.tanh(x * (x2 * (GELU_S * GELU_C) + GELU_S))
    h = 0.5 * t + 0.5
    value = x * h
    return value, h + value * (1.0 - h) * (x2 * (6.0 * GELU_S * GELU_C) + 2.0 * GELU_S)


def load_flow(flow_ref, field, sems):
    cells = field.reshape(2, CHAN * (CX + 2), CY, 128)

    def copy(block, h, c):
        levels = pl.ds(8 * block, 8)
        return pltpu.make_async_copy(
            flow_ref.at[pl.ds(CX * c, CX), levels, pl.ds(128 * h, 128)],
            cells.at[h, pl.ds((CX + 2) * c + 1, CX), levels],
            sems.at[block, h, c],
        )

    copies = [[[copy(block, h, c) for c in range(CHAN)] for h in range(2)] for block in range(3)]
    for copy in sum(sum(copies, []), []):
        copy.start()
    return copies


def level_of(field, h, y):
    return jnp.concatenate(
        [field[h, pl.ds(SLAB * c + CY + y, CX, stride=CY), :] for c in range(CHAN)], 0
    )


def upright(block, h, field, turned):
    for y in range(8 * block, 8 * block + 8):
        turned[pl.ds(y * CZ + 128 * h, 128), :] = level_of(field, h, y).T


def cut(patches, corners_ref, turned, pieces):
    upper = iota((8, 128), 0) < 4
    even = iota((8, 128), 1) % 32 < 16
    for p in patches:
        x0, y0, z0 = corners_ref[0, 0, p], corners_ref[1, 0, p], corners_ref[2, 0, p]
        base = y0 * CZ + z0
        back = lax.rem(128 - x0, 128)
        for pair in range(8):
            halves = []
            for cy in (0, 2):
                both = []
                for parity in range(2):
                    fy, fz = divmod(2 * pair + parity, 4)
                    first = base + (4 * cy + fy) * CZ + fz
                    a = turned[pl.ds(first, 8, stride=4), :]
                    b = turned[pl.ds(first + 4 * CZ - 16, 8, stride=4), :]
                    both.append(
                        pltpu.roll(jnp.where(upper, a, b), back + 16 * parity, 1)
                    )
                halves.append(jnp.where(even, both[0], both[1]))
            pieces[pl.ds(16 * p, 16), pl.ds(128 * pair, 128)] = jnp.concatenate(halves, 0).astype(BF16)


def make_order(order):
    for block in range(8):
        k = iota((128, 1), 0)
        c, parity, cx, fx = k // 32, k // 16 % 2, k // 4 % 4, k % 4
        fyz = 2 * block + parity
        target = cx * FEAT + c * 64 + fx * 16 + fyz
        hit = iota((128, 4 * FEAT), 1) == target
        order[pl.ds(128 * block, 128), :] = jnp.where(hit, 1.0, 0.0).astype(BF16)


def order_rows(half, pieces, order, rows, rows_t):
    tiles = range(4 * half, 4 * half + 4)
    for cx in range(4):
        got = jnp.dot(
            pieces[pl.ds(256 * half, 256), :],
            order[:, pl.ds(FEAT * cx, FEAT)],
            preferred_element_type=F32,
        ).astype(BF16)
        for n, t in enumerate(tiles):
            rows[pl.ds(256 * t + 64 * cx, 64), :] = got[64 * n : 64 * n + 64]
    for t in tiles:
        rows_t[:, pl.ds(256 * t, 256)] = rows[pl.ds(256 * t, 256), :].T


def forward(t, rows, embed, mixer, act, act_t, slope1, slope2, pooled):
    at = pl.ds(t * 256, 256)
    for n in range(2):
        columns = pl.ds(256 * n, 256)
        pre = jnp.dot(rows[at, :], embed[:, columns], preferred_element_type=F32)
        value, slope = gelu_and_slope(pre)
        value = value.astype(BF16)
        act[at, columns] = value
        act_t[columns, at] = value.T
        slope1[at, columns] = slope
    for n in range(2):
        columns = pl.ds(256 * n, 256)
        pre = jnp.dot(act[at, :], mixer[:, columns], preferred_element_type=F32)
        value, slope = gelu_and_slope(pre)
        slope2[at, columns] = slope
        value = value.reshape(4, 4, 16, 256).sum(axis=0).sum(axis=1)
        pooled[t, :, columns] = value * (1.0 / 64)


def head_step(tiles, pooled_ref, goals_ref, learner_ref, head_ref, back, head_grad, slot_part):
    some, first = 4 * len(tiles), 4 * tiles[0]
    pooled = pooled_ref[pl.ds(tiles[0], len(tiles))].reshape(some, HID)
    head = head_ref[...]
    patch = iota((some, PB), 0) + first
    other = iota((some, PB), 1)
    learner_row = learner_ref[...]
    learner = jnp.sum(jnp.where(patch == other, learner_row, 0), axis=1, keepdims=True)
    earlier = (learner == learner_row) & (other < patch)
    within = jnp.sum(jnp.where(earlier, 1, 0), axis=1, keepdims=True)
    slot = learner * CAP + within
    place = iota((some, 128), 1) == slot
    total = jnp.zeros((some, HID), F32)
    head_rows, slot_rows = [], []
    for k in range(3):
        weight = head[k : k + 1, :]
        predicted = jnp.sum(pooled * weight, axis=1, keepdims=True)
        goal = goals_ref[k : k + 1, :].astype(F32)
        goal = jnp.sum(jnp.where(patch == other, goal, 0.0), axis=1, keepdims=True)
        misfit = 2.0 * (predicted - goal)
        total = total + misfit * weight
        head_rows.append(jnp.sum(misfit * pooled, axis=0, keepdims=True))
        slot_rows.append(jnp.sum(jnp.where(place, predicted, 0.0), axis=0, keepdims=True))
    back[pl.ds(tiles[0], len(tiles))] = (total * (1.0 / 64)).reshape(len(tiles), 4, HID)
    if first == 0:
        head_grad[...] = jnp.zeros_like(head_grad)
        slot_part[...] = jnp.zeros_like(slot_part)
    for k in range(3):
        head_grad[k : k + 1, :] += head_rows[k][:, 0:256]
        head_grad[k + 3 : k + 4, :] += head_rows[k][:, 256:512]
        slot_part[k : k + 1, :] += slot_rows[k]


def second_layer_back(t, back, slope2, second):
    at = pl.ds(t * 256, 256)
    for n in range(2):
        columns = pl.ds(256 * n, 256)
        slope = slope2[at, columns].reshape(4, 4, 16, 256)
        value = slope * back[t, :, columns][None, :, None, :]
        second[at, columns] = value.reshape(256, 256).astype(BF16)


def first_layer_back(t, second, mixer_t, slope1, first):
    at = pl.ds(t * 256, 256)
    for n in range(2):
        columns = pl.ds(256 * n, 256)
        value = jnp.dot(second[at, :], mixer_t[:, columns], preferred_element_type=F32)
        first[at, columns] = (value * slope1[at, columns]).astype(BF16)


def send_all(axis, source, target, send_sem, recv_sem):
    bx, by = lax.axis_index("bx"), lax.axis_index("by")
    me, size = (by, BY) if axis == "by" else (bx, BX)

    def step(distance, carry):
        peer = lax.rem(me + distance, size)
        pltpu.make_async_remote_copy(
            src_ref=source(peer),
            dst_ref=target,
            send_sem=send_sem,
            recv_sem=recv_sem,
            device_id=(bx, peer) if axis == "by" else (peer, by),
            device_id_type=MESH,
        ).start()
        return carry

    lax.fori_loop(1, size, step, 0)


def wait_all(buffer, sem):
    blocks = buffer.at[pl.ds(0, buffer.shape[0] - 1)]
    pltpu.make_async_copy(blocks, blocks, sem).wait()


def where_am_i():
    bx, by = lax.axis_index("bx"), lax.axis_index("by")
    div, rem = lax.div, lax.rem
    return [div(bx, 2), rem(div(by, 2), 4), div(by, 8) * 2 + rem(bx, 2), rem(by, 2)]


def device_at(place):
    x, y, z, core = place
    return (x * 2 + lax.rem(z, 2), lax.div(z, 2) * 8 + y * 2 + core)


PLANES = ((0, 1), (1, 2), (2, 0))
LINES = (2, 0, 1)


def plane_peers(job):
    place = where_am_i()
    first, second = PLANES[job]
    turns = [[lax.rem(place[axis] + d, 4) for d in range(4)] for axis in (first, second)]
    peers = []
    for d in (10, 6, 14, 9, 11, 2, 8, 5, 7, 13, 15, 1, 3, 4, 12, 0):
        for other in (0, 1) if job == 2 else (0,):
            if d == 0 and other == 0:
                continue
            there = list(place)
            there[first], there[second] = turns[0][d // 4], turns[1][d % 4]
            block = there[first] * 4 + there[second]
            if other:
                there[3] = 1 - place[3]
            if job == 2:
                block = block + 16 * there[3]
            peers.append((block, device_at(there)))
    return peers


def plane_index(job):
    place = where_am_i()
    first, second = PLANES[job]
    block = place[first] * 4 + place[second]
    return block + 16 * place[3] if job == 2 else block


def mate():
    place = where_am_i()
    place[3] = 1 - place[3]
    return device_at(place)


def partners():
    found = set()
    for y in range(4):
        for z in (0, 2):
            found.update((0, y, z, core) for core in (0, 1))
    for job in range(3):
        for d in range(16):
            there = [0, 0, 0, 0]
            there[PLANES[job][0]], there[PLANES[job][1]] = d // 4, d % 4
            for core in (0, 1) if job == 2 else (0,):
                there[3] = core
                found.add(tuple(there))
    return sorted(found - {(0, 0, 0, 0)})


def greet():
    barrier = pltpu.get_barrier_semaphore()
    here = where_am_i()
    turns = [[lax.rem(here[axis] + d, 4) for d in range(4)] for axis in range(3)]
    for x, y, z, core in partners():
        device = device_at((turns[0][x], turns[1][y], turns[2][z], 1 - here[3] if core else here[3]))
        pl.semaphore_signal(barrier, inc=1, device_id=device, device_id_type=MESH)


def send_plane(job, source, target, sems):
    for n, device in plane_peers(job):
        pltpu.make_async_remote_copy(
            src_ref=source(n),
            dst_ref=target,
            send_sem=sems[0],
            recv_sem=sems[1],
            device_id=device,
            device_id_type=MESH,
        ).start()


def send_line(axis, block, sems):
    for distance in (2, 1, 3):
        place = where_am_i()
        place[axis] = lax.rem(place[axis] + distance, 4)
        pltpu.make_async_remote_copy(
            src_ref=block,
            dst_ref=block,
            send_sem=sems[0],
            recv_sem=sems[1],
            device_id=device_at(place),
            device_id_type=MESH,
        ).start()


def send_mate(source, target, sems):
    pltpu.make_async_remote_copy(
        src_ref=source,
        dst_ref=target,
        send_sem=sems[0],
        recv_sem=sems[1],
        device_id=mate(),
        device_id_type=MESH,
    ).start()


def wait_one(buffer, sem):
    pltpu.make_async_copy(buffer, buffer, sem).wait()


def fill_faces(field, x_face, y_face):
    for h in range(2):
        for side, x in ((0, 0), (1, CX - 1)):
            layers = [field[h, pl.ds(SLAB * c + CY * (x + 1), CY), :] for c in range(CHAN)]
            x_face[side, h] = jnp.concatenate(layers, 0).astype(BF16)
        for side, y in ((0, 0), (1, CY - 1)):
            y_face[side, h] = level_of(field, h, y).astype(BF16)


def halo_copies(x_face, y_face, x_halo, y_halo, send_sems, recv_sems):
    bx, by = lax.axis_index("bx"), lax.axis_index("by")
    copies = []
    for n, (face, halo, device) in enumerate(
        (
            (x_face.at[1], x_halo.at[0], (lax.rem(bx + 1, BX), by)),
            (x_face.at[0], x_halo.at[1], (lax.rem(bx + BX - 1, BX), by)),
            (y_face.at[1], y_halo.at[0], (bx, lax.rem(by + 1, BY))),
            (y_face.at[0], y_halo.at[1], (bx, lax.rem(by + BY - 1, BY))),
        )
    ):
        copies.append(
            pltpu.make_async_remote_copy(
                src_ref=face,
                dst_ref=halo,
                send_sem=send_sems.at[n],
                recv_sem=recv_sems.at[n],
                device_id=device,
                device_id_type=MESH,
            )
        )
    return copies


def place_halos(x_halo, y_halo, field, y_edge):
    for h in range(2):
        for side, slot in ((0, 0), (1, CX + 1)):
            layers = x_halo[side, h].astype(F32)
            for c in range(CHAN):
                rows = pl.ds(SLAB * c + CY * slot, CY)
                field[h, rows, :] = layers[CY * c : CY * c + CY]
            y_edge[side, h] = y_halo[side, h].astype(F32)


def diffuse(c, field, y_edge, moved):
    row, lane = iota((CY, 128), 0), iota((CY, 128), 1)

    def column(x, carry):
        first = SLAB * c + CY + CY * x
        here = pl.ds(pl.multiple_of(first, 8), CY)
        cells = [field[h, here, :] for h in range(2)]
        down = [pltpu.roll(cells[h], 1, 1) for h in range(2)]
        up = [pltpu.roll(cells[h], 127, 1) for h in range(2)]
        below = [jnp.where(lane == 0, 0.0, down[0]), jnp.where(lane == 0, down[0], down[1])]
        above = [jnp.where(lane == 127, up[1], up[0]), jnp.where(lane == 127, 0.0, up[1])]
        for h in range(2):
            total = below[h] + above[h]
            total = total + field[h, pl.ds(pl.multiple_of(first - CY, 8), CY), :]
            total = total + field[h, pl.ds(pl.multiple_of(first + CY, 8), CY), :]
            low = y_edge[0, h, pl.ds(CX * c + x, 1), :]
            high = y_edge[1, h, pl.ds(CX * c + x, 1), :]
            total = total + jnp.where(row == 0, low, field[h, pl.ds(first - 1, CY), :])
            total = total + jnp.where(row == CY - 1, high, field[h, pl.ds(first + 1, CY), :])
            rows = pl.ds(pl.multiple_of(CX * CY * c + CY * x, 8), CY)
            moved[rows, pl.ds(128 * h, 128)] = (1.0 - 6.0 * KAPPA) * cells[h] + KAPPA * total
        return carry

    lax.fori_loop(0, CX, column, 0, unroll=8)


def sum_blocks(buffer, count):
    total = buffer[0].astype(F32)
    for n in range(1, count):
        total = total + buffer[n].astype(F32)
    return total


def read_slots(slot_got):
    by = lax.axis_index("by")
    lane = iota((8, 128), 1)
    total = jnp.zeros((8, 128), F32)
    for j in range(BY):
        block = pltpu.roll(slot_got[j], lax.rem(128 + CAP * j - CAP * by, 128), 1)
        total = jnp.where(lane // CAP == j, block, total)
    return total


PAIR, PLANE, LINE, PLANE_ALL, MATE = range(5)


def step_kernel(
    corners_in, flow_ref, learner_in, goals_in, embed_ref, mixer_ref, head_in,
    moved, full, full_e, head_total, slots,
    corners_ref, learner_ref, goals_ref, head_ref, field, turned, pieces, order, rows, embed_wide, mixer_wide, embed, mixer, mixer_t, act, slope1,
    slope2, pooled, back, second, first, rows_t, act_t, mixer_early, embed_early, x_face, y_face, x_halo, y_halo, y_edge,
    head_grad, head_pair, head_got, slot_part, slot_got, own, pair_got, part, plane_got, line_got, part_e, plane_got_e,
    load_sems, weight_sems, halo_send, halo_recv, slot_sems, head_send, head_recv, job_send, job_recv,
):
    bx, by = lax.axis_index("bx"), lax.axis_index("by")
    core = lax.rem(by, 2)
    loads = load_flow(flow_ref, field, load_sems)
    corners = pltpu.make_async_copy(corners_in, corners_ref, weight_sems.at[0])
    corners.start()
    weights = [
        pltpu.make_async_copy(source, target, weight_sems.at[n + 1])
        for n, (source, target) in enumerate(
            (
                (embed_ref, embed_wide), (mixer_ref, mixer_wide), (learner_in, learner_ref),
                (goals_in, goals_ref), (head_in, head_ref),
            )
        )
    ]
    for copy in weights:
        copy.start()
    greet()
    make_order(order)
    for block in range(3):
        for h in range(2):
            for copy in loads[block][h]:
                copy.wait()
            upright(block, h, field, turned)
    early, late = pl.ds(0, 256 * EARLY), pl.ds(256 * EARLY, 256 * (TILES - EARLY))

    def product(turned_rows, columns, along, factor):
        return jnp.dot(turned_rows[columns, along], factor[along, :], preferred_element_type=F32)

    corners.wait()
    cut(range(0, 16), corners_ref, turned, pieces)
    for copy in weights:
        copy.wait()
    order_rows(0, pieces, order, rows, rows_t)
    embed[...] = embed_wide[...].astype(BF16)
    mixer[...] = mixer_wide[...].astype(BF16)
    mixer_t[...] = mixer_wide[...].T.astype(BF16)
    fill_faces(field, x_face, y_face)
    pl.semaphore_wait(pltpu.get_barrier_semaphore(), len(partners()))
    halos = halo_copies(x_face, y_face, x_halo, y_halo, halo_send, halo_recv)
    for copy in halos:
        copy.start()
    for t in range(4):
        forward(t, rows, embed, mixer, act, act_t, slope1, slope2, pooled)
        cut(range(16 + 4 * t, 20 + 4 * t), corners_ref, turned, pieces)
    order_rows(1, pieces, order, rows, rows_t)
    for t in range(4, TILES):
        forward(t, rows, embed, mixer, act, act_t, slope1, slope2, pooled)
        if t == EARLY - 1:
            head_step(range(EARLY), pooled, goals_ref, learner_ref, head_ref, back, head_grad, slot_part)
        if t >= EARLY:
            for n in range(3 * (t - EARLY), 3 * (t - EARLY) + 3):
                second_layer_back(n, back, slope2, second)
                first_layer_back(n, second, mixer_t, slope1, first)
    head_step(range(EARLY, TILES), pooled, goals_ref, learner_ref, head_ref, back, head_grad, slot_part)
    for half in range(2):
        part_of = pl.ds(256 * half, 256)
        mixer_early[part_of, :] = product(act_t, part_of, early, second)
    embed_early[...] = product(rows_t, pl.ds(0, FEAT), early, first)

    send_mate(head_grad, head_pair, (head_send.at[0], head_recv.at[0]))

    def head_line(axis, value):
        me = where_am_i()[axis]
        block = head_got.at[axis, me]
        block[...] = value
        send_line(axis, block, (head_send.at[axis + 1], head_recv.at[axis + 1]))

    def head_line_sum(axis):
        wait_all(head_got.at[axis], head_recv.at[axis + 1])
        return sum_blocks(head_got.at[axis], 4)

    def sems(job, group):
        return job_send.at[job, group], job_recv.at[job, group]

    def start_pair(job, gradient):
        own[job] = gradient.reshape(2, 128, HID).astype(BF16)
        send_mate(own.at[job, 1 - core], pair_got.at[job], sems(job, PAIR))

    parts = (part.at[0], part.at[1], part_e)
    gots = (plane_got.at[0], plane_got.at[1], plane_got_e)
    fulls = (full.at[0, core], full.at[1, core], full_e)

    def plane_sends(job):
        me = plane_index(job)
        send_plane(job, lambda n: parts[job].at[n], gots[job].at[me], sems(job, PLANE))
        gots[job][me] = parts[job][me]

    def start_plane(job):
        wait_one(pair_got.at[job], job_recv.at[job, PAIR])
        total = (own[job, core].astype(F32) + pair_got[job].astype(F32)).astype(BF16)
        for n in range(16):
            part[job, n] = total[16 * (n // 2) : 16 * (n // 2) + 16, 256 * (n % 2) : 256 * (n % 2) + 256]
        plane_sends(job)

    def start_plane_e(gradient):
        total = gradient.astype(BF16)
        for n in range(32):
            part_e[n] = total[16 * (n // 2) : 16 * (n // 2) + 16, 256 * (n % 2) : 256 * (n % 2) + 256]
        plane_sends(2)

    def start_line(job):
        wait_all(gots[job], job_recv.at[job, PLANE])
        me = where_am_i()[LINES[job]]
        line_got[job, me] = sum_blocks(gots[job], gots[job].shape[0]).astype(BF16)
        send_line(LINES[job], line_got.at[job, me], sems(job, LINE))

    def start_plane_all(job):
        wait_all(line_got.at[job], job_recv.at[job, LINE])
        block = fulls[job].at[plane_index(job)]
        block[...] = sum_blocks(line_got.at[job], 4).astype(BF16)
        send_plane(job, lambda n: block, block, sems(job, PLANE_ALL))

    def start_mate(job):
        wait_all(fulls[job], job_recv.at[job, PLANE_ALL])
        send_mate(fulls[job], fulls[job], sems(job, MATE))

    for t in range(EARLY, TILES):
        second_layer_back(t, back, slope2, second)
    for half in range(2):
        part_of = pl.ds(256 * half, 256)
        start_pair(half, mixer_early[part_of, :] + product(act_t, part_of, late, second))
    for t in range(EARLY, TILES):
        first_layer_back(t, second, mixer_t, slope1, first)
    start_plane_e(embed_early[...] + product(rows_t, pl.ds(0, FEAT), late, first))
    start_plane(0)
    start_plane(1)

    wait_one(head_pair, head_recv.at[0])
    head_line(1, head_grad[...] + head_pair[...])
    for copy in halos:
        copy.wait()
    place_halos(x_halo, y_halo, field, y_edge)
    start_line(0)
    start_line(1)
    head_line(2, head_line_sum(1))
    send_all("by", lambda peer: slot_part, slot_got.at[by], slot_sems.at[0], slot_sems.at[1])
    slot_got[by] = slot_part[...]
    diffuse(0, field, y_edge, moved)
    start_plane_all(0)
    start_plane_all(1)
    start_line(2)
    head_line(0, head_line_sum(2))
    diffuse(1, field, y_edge, moved)
    start_plane_all(2)
    wait_all(slot_got, slot_sems.at[1])
    slots[...] = read_slots(slot_got)
    diffuse(2, field, y_edge, moved)
    start_mate(0)
    start_mate(1)
    diffuse(3, field, y_edge, moved)
    head_total[...] = head_line_sum(0)
    wait_all(full_e, job_recv.at[2, PLANE_ALL])
    for job in range(2):
        wait_one(full.at[job, 1 - core], job_recv.at[job, MATE])
    wait_all(slot_got, slot_sems.at[0])
    wait_one(head_pair, head_send.at[0])
    for axis in range(3):
        wait_all(head_got.at[axis], head_send.at[axis + 1])
    for job in range(3):
        wait_all(gots[job], job_send.at[job, PLANE])
        wait_all(line_got.at[job], job_send.at[job, LINE])
        wait_all(fulls[job], job_send.at[job, PLANE_ALL])
    for job in range(2):
        wait_one(pair_got.at[job], job_send.at[job, PAIR])
        wait_one(fulls[job], job_send.at[job, MATE])


def scale_of(square_sum, count):
    return lax.rsqrt(jnp.sum(square_sum, keepdims=True) * (1.0 / count) + EPSILON)


def write_sum(blocks, wide, out, sems):
    total = jnp.zeros((16, 256), F32)
    for block in blocks:
        value = block[...].astype(F32)
        total = total + value * value
    scale = scale_of(total, len(blocks) * 16 * 256)
    copies = []
    for n, block in enumerate(blocks):
        wide[pl.ds(16 * (n // 2), 16), pl.ds(256 * (n % 2), 256)] = block[...].astype(F32) * scale
        if n % 16 == 15:
            rows = pl.ds(128 * (n // 16), 128)
            copies.append(pltpu.make_async_copy(wide.at[rows], out.at[rows], sems.at[n // 16]))
            copies[-1].start()
    return copies


def finish_kernel(
    moved, full, full_e, head_total, slots, flow_out, slot_out, embed_out, mixer_out, head_out,
    slot_wide, head_wide, embed_wide, mixer_wide, flow_sems, small_sems, embed_sems, mixer_sems,
):
    copies = []
    for n in range(8):
        part = pl.ds(COLS // 8 * n, COLS // 8)
        copies.append(pltpu.make_async_copy(moved.at[part], flow_out.at[part], flow_sems.at[n]))
    for copy in copies:
        copy.start()
    total = head_total[...]
    total = total * scale_of(total * total, 3 * HID)
    for k in range(3):
        head_wide[k : k + 1, 0:256] = total[k : k + 1]
        head_wide[k : k + 1, 256:512] = total[k + 3 : k + 4]
        slot_wide[k] = slots[k : k + 1, 0:64]
    for n, (source, target) in enumerate(((slot_wide, slot_out), (head_wide, head_out))):
        copies.append(pltpu.make_async_copy(source, target, small_sems.at[n]))
        copies[-1].start()
    copies += write_sum(
        [full.at[j, h, n] for j in range(2) for h in range(2) for n in range(16)],
        mixer_wide, mixer_out, mixer_sems,
    )
    copies += write_sum([full_e.at[n] for n in range(32)], embed_wide, embed_out, embed_sems)
    for copy in copies:
        copy.wait()


SCRATCH = [
    pltpu.SMEM((3, 1, PB), jnp.int32),
    pltpu.VMEM((1, PB), jnp.int32),
    pltpu.VMEM((3, PB), BF16),
    pltpu.VMEM((3, HID), F32),
    pltpu.VMEM((2, CHAN * SLAB, 128), F32),
    pltpu.VMEM((CY * CZ + 32, 128), F32),
    pltpu.VMEM((512, 1024), BF16),
    pltpu.VMEM((1024, 1024), BF16),
    pltpu.VMEM((2048, FEAT), BF16),
    pltpu.VMEM((FEAT, HID), F32),
    pltpu.VMEM((HID, HID), F32),
    pltpu.VMEM((FEAT, HID), BF16),
    pltpu.VMEM((HID, HID), BF16),
    pltpu.VMEM((HID, HID), BF16),
    pltpu.VMEM((2048, HID), BF16),
    pltpu.VMEM((2048, HID), F32),
    pltpu.VMEM((2048, HID), F32),
    pltpu.VMEM((TILES, 4, HID), F32),
    pltpu.VMEM((TILES, 4, HID), F32),
    pltpu.VMEM((2048, HID), BF16),
    pltpu.VMEM((2048, HID), BF16),
    pltpu.VMEM((FEAT, 2048), BF16),
    pltpu.VMEM((HID, 2048), BF16),
    pltpu.VMEM((HID, HID), F32),
    pltpu.VMEM((FEAT, HID), F32),
    pltpu.VMEM((2, 2, CHAN * CY, 128), BF16),
    pltpu.VMEM((2, 2, CHAN * CX, 128), BF16),
    pltpu.VMEM((2, 2, CHAN * CY, 128), BF16),
    pltpu.VMEM((2, 2, CHAN * CX, 128), BF16),
    pltpu.VMEM((2, 2, CHAN * CX, 128), F32),
    pltpu.VMEM((8, 256), F32),
    pltpu.VMEM((8, 256), F32),
    pltpu.VMEM((3, 4, 8, 256), F32),
    pltpu.VMEM((8, 128), F32),
    pltpu.VMEM((BY, 8, 128), F32),
    pltpu.VMEM((2, 2, 128, HID), BF16),
    pltpu.VMEM((2, 128, HID), BF16),
    pltpu.VMEM((2, 16, 16, 256), BF16),
    pltpu.VMEM((2, 16, 16, 256), BF16),
    pltpu.VMEM((3, 4, 16, 256), BF16),
    pltpu.VMEM((32, 16, 256), BF16),
    pltpu.VMEM((32, 16, 256), BF16),
    pltpu.SemaphoreType.DMA((3, 2, CHAN)),
    pltpu.SemaphoreType.DMA((6,)),
    pltpu.SemaphoreType.DMA((4,)),
    pltpu.SemaphoreType.DMA((4,)),
    pltpu.SemaphoreType.DMA((2,)),
    pltpu.SemaphoreType.DMA((4,)),
    pltpu.SemaphoreType.DMA((4,)),
    pltpu.SemaphoreType.DMA((3, 5)),
    pltpu.SemaphoreType.DMA((3, 5)),
]


def per_device(
    flow_field, patch_corners, patch_learner, drag_target, embed_weight, mixer_weight, head_weight
):
    vmem = pl.BlockSpec(memory_space=pltpu.VMEM)
    anywhere = pl.BlockSpec(memory_space=pl.ANY)
    parts = pl.pallas_call(
        step_kernel,
        out_shape=(
            pltpu.VMEM((COLS, CZ), F32),
            pltpu.VMEM((2, 2, 16, 16, 256), BF16),
            pltpu.VMEM((32, 16, 256), BF16),
            pltpu.VMEM((8, 256), F32),
            pltpu.VMEM((8, 128), F32),
        ),
        in_specs=[anywhere] * 7,
        out_specs=(vmem,) * 5,
        scratch_shapes=SCRATCH,
        compiler_params=pltpu.CompilerParams(
            collective_id=0, has_side_effects=True, vmem_limit_bytes=44 * 2**20
        ),
    )(
        *(
            pltpu.with_memory_space_constraint(value, pltpu.HBM)
            for value in (
                patch_corners, flow_field.reshape(CHAN * CX, CY, CZ), patch_learner.reshape(1, PB),
                drag_target.reshape(3, PB), embed_weight, mixer_weight, head_weight,
            )
        )
    )
    flow, slots, embed, mixer, head = pl.pallas_call(
        finish_kernel,
        out_shape=(
            jax.ShapeDtypeStruct((COLS, CZ), F32),
            jax.ShapeDtypeStruct((3, 1, 64), F32),
            jax.ShapeDtypeStruct((FEAT, HID), F32),
            jax.ShapeDtypeStruct((HID, HID), F32),
            jax.ShapeDtypeStruct((3, HID), F32),
        ),
        in_specs=[vmem] * 5,
        out_specs=(anywhere,) * 5,
        scratch_shapes=[
            pltpu.VMEM((3, 1, 64), F32),
            pltpu.VMEM((3, HID), F32),
            pltpu.VMEM((FEAT, HID), F32),
            pltpu.VMEM((HID, HID), F32),
            pltpu.SemaphoreType.DMA((8,)),
            pltpu.SemaphoreType.DMA((2,)),
            pltpu.SemaphoreType.DMA((2,)),
            pltpu.SemaphoreType.DMA((4,)),
        ],
        compiler_params=pltpu.CompilerParams(vmem_limit_bytes=16 * 2**20),
    )(*parts)
    return flow.reshape(CHAN, CX, CY, CZ), slots, embed, mixer, head


def solution(mesh):
    return jax.shard_map(
        per_device,
        mesh=mesh,
        in_specs=(
            P(None, "bx", "by", None),
            P(None, "bx", "by"),
            P("bx", "by", None),
            P(None, "bx", "by"),
            P(),
            P(),
            P(),
        ),
        out_specs=(P(None, "bx", "by", None), P(None, "bx", "by"), P(), P(), P()),
        check_vma=False,
    )
```

```python
import functools
import jax
import jax.numpy as jnp
from jax import lax
from jax.experimental import pallas as pl
from jax.experimental.pallas import tpu as pltpu
from jax.sharding import PartitionSpec as P

CHAN, CX, CY, CZ = 4, 32, 24, 256
PB, CAP, HID, FEAT = 32, 4, 512, 256
COLS = CHAN * CX * CY
SLAB = (CX + 2) * CY
BX, BY = 8, 16
MESH = pl.DeviceIdType.MESH
TILES = 8
KAPPA = 0.15
EPSILON = 1e-06
GELU_S = 0.7978845608028654
GELU_C = 0.044715
F32, BF16 = jnp.float32, jnp.bfloat16


def iota(shape, axis):
    return lax.broadcasted_iota(jnp.int32, shape, axis)


def gelu_and_slope(x):
    x2 = x * x
    t = jnp.tanh(x * (x2 * (GELU_S * GELU_C) + GELU_S))
    h = 0.5 * t + 0.5
    value = x * h
    return value, h + value * (1.0 - h) * (x2 * (6.0 * GELU_S * GELU_C) + 2.0 * GELU_S)


def load_flow(flow_ref, field, sems):
    cells = field.reshape(2, CHAN * (CX + 2), CY, 128)

    def copy(block, h, c):
        levels = pl.ds(8 * block, 8)
        return pltpu.make_async_copy(
            flow_ref.at[pl.ds(CX * c, CX), levels, pl.ds(128 * h, 128)],
            cells.at[h, pl.ds((CX + 2) * c + 1, CX), levels],
            sems.at[block, h, c],
        )

    copies = [[[copy(block, h, c) for c in range(CHAN)] for h in range(2)] for block in range(3)]
    for copy in sum(sum(copies, []), []):
        copy.start()
    return copies


def level_of(field, h, y):
    return jnp.concatenate(
        [field[h, pl.ds(SLAB * c + CY + y, CX, stride=CY), :] for c in range(CHAN)], 0
    )


def upright(block, h, field, turned):
    for y in range(8 * block, 8 * block + 8):
        turned[pl.ds(y * CZ + 128 * h, 128), :] = level_of(field, h, y).T


def cut(patches, corners_ref, turned, pieces):
    upper = iota((8, 128), 0) < 4
    even = iota((8, 128), 1) % 32 < 16
    for p in patches:
        x0, y0, z0 = corners_ref[0, 0, p], corners_ref[1, 0, p], corners_ref[2, 0, p]
        base = y0 * CZ + z0
        back = lax.rem(128 - x0, 128)
        for pair in range(8):
            halves = []
            for cy in (0, 2):
                both = []
                for parity in range(2):
                    fy, fz = divmod(2 * pair + parity, 4)
                    first = base + (4 * cy + fy) * CZ + fz
                    a = turned[pl.ds(first, 8, stride=4), :]
                    b = turned[pl.ds(first + 4 * CZ - 16, 8, stride=4), :]
                    both.append(
                        pltpu.roll(jnp.where(upper, a, b), back + 16 * parity, 1)
                    )
                halves.append(jnp.where(even, both[0], both[1]))
            pieces[pl.ds(16 * p, 16), pl.ds(128 * pair, 128)] = jnp.concatenate(halves, 0).astype(BF16)


def make_order(order):
    for block in range(8):
        k = iota((128, 1), 0)
        c, parity, cx, fx = k // 32, k // 16 % 2, k // 4 % 4, k % 4
        fyz = 2 * block + parity
        target = cx * FEAT + c * 64 + fx * 16 + fyz
        hit = iota((128, 4 * FEAT), 1) == target
        order[pl.ds(128 * block, 128), :] = jnp.where(hit, 1.0, 0.0).astype(BF16)


def order_rows(half, pieces, order, rows, rows_t):
    tiles = range(4 * half, 4 * half + 4)
    for cx in range(4):
        got = jnp.dot(
            pieces[pl.ds(256 * half, 256), :],
            order[:, pl.ds(FEAT * cx, FEAT)],
            preferred_element_type=F32,
        ).astype(BF16)
        for n, t in enumerate(tiles):
            rows[pl.ds(256 * t + 64 * cx, 64), :] = got[64 * n : 64 * n + 64]
    for t in tiles:
        rows_t[:, pl.ds(256 * t, 256)] = rows[pl.ds(256 * t, 256), :].T


def forward(t, rows, embed, mixer, act, act_t, slope1, slope2, pooled):
    at = pl.ds(t * 256, 256)
    for n in range(2):
        columns = pl.ds(256 * n, 256)
        pre = jnp.dot(rows[at, :], embed[:, columns], preferred_element_type=F32)
        value, slope = gelu_and_slope(pre)
        value = value.astype(BF16)
        act[at, columns] = value
        act_t[columns, at] = value.T
        slope1[at, columns] = slope
    for n in range(2):
        columns = pl.ds(256 * n, 256)
        pre = jnp.dot(act[at, :], mixer[:, columns], preferred_element_type=F32)
        value, slope = gelu_and_slope(pre)
        slope2[at, columns] = slope
        value = value.reshape(4, 4, 16, 256).sum(axis=0).sum(axis=1)
        pooled[t, :, columns] = value * (1.0 / 64)


def head_step(half, pooled_ref, goals_ref, learner_ref, head_ref, back, head_grad, slot_part):
    some = PB // 2
    first = some * half
    pooled = pooled_ref[pl.ds(4 * half, 4)].reshape(some, HID)
    head = head_ref[...]
    patch = iota((some, PB), 0) + first
    other = iota((some, PB), 1)
    learner_row = learner_ref[...]
    learner = jnp.sum(jnp.where(patch == other, learner_row, 0), axis=1, keepdims=True)
    earlier = (learner == learner_row) & (other < patch)
    within = jnp.sum(jnp.where(earlier, 1, 0), axis=1, keepdims=True)
    slot = learner * CAP + within
    place = iota((some, 128), 1) == slot
    total = jnp.zeros((some, HID), F32)
    head_rows, slot_rows = [], []
    for k in range(3):
        weight = head[k : k + 1, :]
        predicted = jnp.sum(pooled * weight, axis=1, keepdims=True)
        goal = goals_ref[k : k + 1, :].astype(F32)
        goal = jnp.sum(jnp.where(patch == other, goal, 0.0), axis=1, keepdims=True)
        misfit = 2.0 * (predicted - goal)
        total = total + misfit * weight
        head_rows.append(jnp.sum(misfit * pooled, axis=0, keepdims=True))
        slot_rows.append(jnp.sum(jnp.where(place, predicted, 0.0), axis=0, keepdims=True))
    back[pl.ds(4 * half, 4)] = (total * (1.0 / 64)).reshape(4, 4, HID)
    if half == 0:
        head_grad[...] = jnp.zeros_like(head_grad)
        slot_part[...] = jnp.zeros_like(slot_part)
    for k in range(3):
        head_grad[k : k + 1, :] += head_rows[k][:, 0:256]
        head_grad[k + 3 : k + 4, :] += head_rows[k][:, 256:512]
        slot_part[k : k + 1, :] += slot_rows[k]


def second_layer_back(t, back, slope2, second):
    at = pl.ds(t * 256, 256)
    for n in range(2):
        columns = pl.ds(256 * n, 256)
        slope = slope2[at, columns].reshape(4, 4, 16, 256)
        value = slope * back[t, :, columns][None, :, None, :]
        second[at, columns] = value.reshape(256, 256).astype(BF16)


def first_layer_back(t, second, mixer_t, slope1, first):
    at = pl.ds(t * 256, 256)
    for n in range(2):
        columns = pl.ds(256 * n, 256)
        value = jnp.dot(second[at, :], mixer_t[:, columns], preferred_element_type=F32)
        first[at, columns] = (value * slope1[at, columns]).astype(BF16)


def send_all(axis, source, target, send_sem, recv_sem):
    bx, by = lax.axis_index("bx"), lax.axis_index("by")
    me, size = (by, BY) if axis == "by" else (bx, BX)

    def step(distance, carry):
        peer = lax.rem(me + distance, size)
        pltpu.make_async_remote_copy(
            src_ref=source(peer),
            dst_ref=target,
            send_sem=send_sem,
            recv_sem=recv_sem,
            device_id=(bx, peer) if axis == "by" else (peer, by),
            device_id_type=MESH,
        ).start()
        return carry

    lax.fori_loop(1, size, step, 0)


def wait_all(buffer, sem):
    blocks = buffer.at[pl.ds(0, buffer.shape[0] - 1)]
    pltpu.make_async_copy(blocks, blocks, sem).wait()


def where_am_i():
    bx, by = lax.axis_index("bx"), lax.axis_index("by")
    div, rem = lax.div, lax.rem
    return [div(bx, 2), rem(div(by, 2), 4), div(by, 8) * 2 + rem(bx, 2), rem(by, 2)]


def device_at(place):
    x, y, z, core = place
    return (x * 2 + lax.rem(z, 2), lax.div(z, 2) * 8 + y * 2 + core)


PLANES = ((0, 1), (1, 2), (2, 0))
LINES = (2, 0, 1)


def plane_peers(job):
    place = where_am_i()
    first, second = PLANES[job]
    turns = [[lax.rem(place[axis] + d, 4) for d in range(4)] for axis in (first, second)]
    peers = []
    for d in (10, 6, 14, 9, 11, 2, 8, 5, 7, 13, 15, 1, 3, 4, 12, 0):
        for other in (0, 1) if job == 2 else (0,):
            if d == 0 and other == 0:
                continue
            there = list(place)
            there[first], there[second] = turns[0][d // 4], turns[1][d % 4]
            block = there[first] * 4 + there[second]
            if other:
                there[3] = 1 - place[3]
            if job == 2:
                block = block + 16 * there[3]
            peers.append((block, device_at(there)))
    return peers


def plane_index(job):
    place = where_am_i()
    first, second = PLANES[job]
    block = place[first] * 4 + place[second]
    return block + 16 * place[3] if job == 2 else block


def mate():
    place = where_am_i()
    place[3] = 1 - place[3]
    return device_at(place)


def partners():
    found = set()
    for y in range(4):
        for z in (0, 2):
            found.update((0, y, z, core) for core in (0, 1))
    for job in range(3):
        for d in range(16):
            there = [0, 0, 0, 0]
            there[PLANES[job][0]], there[PLANES[job][1]] = d // 4, d % 4
            for core in (0, 1) if job == 2 else (0,):
                there[3] = core
                found.add(tuple(there))
    return sorted(found - {(0, 0, 0, 0)})


def greet():
    barrier = pltpu.get_barrier_semaphore()
    here = where_am_i()
    turns = [[lax.rem(here[axis] + d, 4) for d in range(4)] for axis in range(3)]
    for x, y, z, core in partners():
        device = device_at((turns[0][x], turns[1][y], turns[2][z], 1 - here[3] if core else here[3]))
        pl.semaphore_signal(barrier, inc=1, device_id=device, device_id_type=MESH)


def send_plane(job, source, target, sems):
    for n, device in plane_peers(job):
        pltpu.make_async_remote_copy(
            src_ref=source(n),
            dst_ref=target,
            send_sem=sems[0],
            recv_sem=sems[1],
            device_id=device,
            device_id_type=MESH,
        ).start()


def send_line(axis, block, sems):
    for distance in (2, 1, 3):
        place = where_am_i()
        place[axis] = lax.rem(place[axis] + distance, 4)
        pltpu.make_async_remote_copy(
            src_ref=block,
            dst_ref=block,
            send_sem=sems[0],
            recv_sem=sems[1],
            device_id=device_at(place),
            device_id_type=MESH,
        ).start()


def send_mate(source, target, sems):
    pltpu.make_async_remote_copy(
        src_ref=source,
        dst_ref=target,
        send_sem=sems[0],
        recv_sem=sems[1],
        device_id=mate(),
        device_id_type=MESH,
    ).start()


def wait_one(buffer, sem):
    pltpu.make_async_copy(buffer, buffer, sem).wait()


def fill_faces(field, x_face, y_face):
    for h in range(2):
        for side, x in ((0, 0), (1, CX - 1)):
            layers = [field[h, pl.ds(SLAB * c + CY * (x + 1), CY), :] for c in range(CHAN)]
            x_face[side, h] = jnp.concatenate(layers, 0).astype(BF16)
        for side, y in ((0, 0), (1, CY - 1)):
            y_face[side, h] = level_of(field, h, y).astype(BF16)


def halo_copies(x_face, y_face, x_halo, y_halo, send_sems, recv_sems):
    bx, by = lax.axis_index("bx"), lax.axis_index("by")
    copies = []
    for n, (face, halo, device) in enumerate(
        (
            (x_face.at[1], x_halo.at[0], (lax.rem(bx + 1, BX), by)),
            (x_face.at[0], x_halo.at[1], (lax.rem(bx + BX - 1, BX), by)),
            (y_face.at[1], y_halo.at[0], (bx, lax.rem(by + 1, BY))),
            (y_face.at[0], y_halo.at[1], (bx, lax.rem(by + BY - 1, BY))),
        )
    ):
        copies.append(
            pltpu.make_async_remote_copy(
                src_ref=face,
                dst_ref=halo,
                send_sem=send_sems.at[n],
                recv_sem=recv_sems.at[n],
                device_id=device,
                device_id_type=MESH,
            )
        )
    return copies


def place_halos(x_halo, y_halo, field, y_edge):
    for h in range(2):
        for side, slot in ((0, 0), (1, CX + 1)):
            layers = x_halo[side, h].astype(F32)
            for c in range(CHAN):
                rows = pl.ds(SLAB * c + CY * slot, CY)
                field[h, rows, :] = layers[CY * c : CY * c + CY]
            y_edge[side, h] = y_halo[side, h].astype(F32)


def diffuse(c, field, y_edge, moved):
    row, lane = iota((CY, 128), 0), iota((CY, 128), 1)

    def column(x, carry):
        first = SLAB * c + CY + CY * x
        here = pl.ds(pl.multiple_of(first, 8), CY)
        cells = [field[h, here, :] for h in range(2)]
        down = [pltpu.roll(cells[h], 1, 1) for h in range(2)]
        up = [pltpu.roll(cells[h], 127, 1) for h in range(2)]
        below = [jnp.where(lane == 0, 0.0, down[0]), jnp.where(lane == 0, down[0], down[1])]
        above = [jnp.where(lane == 127, up[1], up[0]), jnp.where(lane == 127, 0.0, up[1])]
        for h in range(2):
            total = below[h] + above[h]
            total = total + field[h, pl.ds(pl.multiple_of(first - CY, 8), CY), :]
            total = total + field[h, pl.ds(pl.multiple_of(first + CY, 8), CY), :]
            low = y_edge[0, h, pl.ds(CX * c + x, 1), :]
            high = y_edge[1, h, pl.ds(CX * c + x, 1), :]
            total = total + jnp.where(row == 0, low, field[h, pl.ds(first - 1, CY), :])
            total = total + jnp.where(row == CY - 1, high, field[h, pl.ds(first + 1, CY), :])
            rows = pl.ds(pl.multiple_of(CX * CY * c + CY * x, 8), CY)
            moved[rows, pl.ds(128 * h, 128)] = (1.0 - 6.0 * KAPPA) * cells[h] + KAPPA * total
        return carry

    lax.fori_loop(0, CX, column, 0, unroll=8)


def sum_blocks(buffer, count):
    total = buffer[0].astype(F32)
    for n in range(1, count):
        total = total + buffer[n].astype(F32)
    return total


def read_slots(slot_got):
    by = lax.axis_index("by")
    lane = iota((8, 128), 1)
    total = jnp.zeros((8, 128), F32)
    for j in range(BY):
        block = pltpu.roll(slot_got[j], lax.rem(128 + CAP * j - CAP * by, 128), 1)
        total = jnp.where(lane // CAP == j, block, total)
    return total


PAIR, PLANE, LINE, PLANE_ALL, MATE = range(5)


def step_kernel(
    corners_in, flow_ref, learner_in, goals_in, embed_ref, mixer_ref, head_in,
    moved, full, full_e, head_total, slots,
    corners_ref, learner_ref, goals_ref, head_ref, field, turned, pieces, order, rows, embed_wide, mixer_wide, embed, mixer, mixer_t, act, slope1,
    slope2, pooled, back, second, first, rows_t, act_t, mixer_early, x_face, y_face, x_halo, y_halo, y_edge,
    head_grad, head_pair, head_got, slot_part, slot_got, own, pair_got, part, plane_got, line_got, part_e, plane_got_e,
    load_sems, weight_sems, halo_send, halo_recv, slot_sems, head_send, head_recv, job_send, job_recv,
):
    bx, by = lax.axis_index("bx"), lax.axis_index("by")
    core = lax.rem(by, 2)
    loads = load_flow(flow_ref, field, load_sems)
    corners = pltpu.make_async_copy(corners_in, corners_ref, weight_sems.at[0])
    corners.start()
    weights = [
        pltpu.make_async_copy(source, target, weight_sems.at[n + 1])
        for n, (source, target) in enumerate(
            (
                (embed_ref, embed_wide), (mixer_ref, mixer_wide), (learner_in, learner_ref),
                (goals_in, goals_ref), (head_in, head_ref),
            )
        )
    ]
    for copy in weights:
        copy.start()
    greet()
    make_order(order)
    for block in range(3):
        for h in range(2):
            for copy in loads[block][h]:
                copy.wait()
            upright(block, h, field, turned)
    early, late = pl.ds(0, 1024), pl.ds(1024, 1024)

    def product(turned_rows, columns, along, factor):
        return jnp.dot(turned_rows[columns, along], factor[along, :], preferred_element_type=F32)

    corners.wait()
    cut(range(0, 16), corners_ref, turned, pieces)
    for copy in weights:
        copy.wait()
    order_rows(0, pieces, order, rows, rows_t)
    embed[...] = embed_wide[...].astype(BF16)
    mixer[...] = mixer_wide[...].astype(BF16)
    mixer_t[...] = mixer_wide[...].T.astype(BF16)
    fill_faces(field, x_face, y_face)
    pl.semaphore_wait(pltpu.get_barrier_semaphore(), len(partners()))
    halos = halo_copies(x_face, y_face, x_halo, y_halo, halo_send, halo_recv)
    for copy in halos:
        copy.start()
    for t in range(4):
        forward(t, rows, embed, mixer, act, act_t, slope1, slope2, pooled)
        cut(range(16 + 4 * t, 20 + 4 * t), corners_ref, turned, pieces)
    order_rows(1, pieces, order, rows, rows_t)
    head_step(0, pooled, goals_ref, learner_ref, head_ref, back, head_grad, slot_part)
    for t in range(4, 8):
        forward(t, rows, embed, mixer, act, act_t, slope1, slope2, pooled)
        second_layer_back(t - 4, back, slope2, second)
    head_step(1, pooled, goals_ref, learner_ref, head_ref, back, head_grad, slot_part)
    for half in range(2):
        part_of = pl.ds(256 * half, 256)
        mixer_early[part_of, :] = product(act_t, part_of, early, second)

    send_mate(head_grad, head_pair, (head_send.at[0], head_recv.at[0]))

    def head_line(axis, value):
        me = where_am_i()[axis]
        block = head_got.at[axis, me]
        block[...] = value
        send_line(axis, block, (head_send.at[axis + 1], head_recv.at[axis + 1]))

    def head_line_sum(axis):
        wait_all(head_got.at[axis], head_recv.at[axis + 1])
        return sum_blocks(head_got.at[axis], 4)

    def sems(job, group):
        return job_send.at[job, group], job_recv.at[job, group]

    def start_pair(job, gradient):
        own[job] = gradient.reshape(2, 128, HID).astype(BF16)
        send_mate(own.at[job, 1 - core], pair_got.at[job], sems(job, PAIR))

    parts = (part.at[0], part.at[1], part_e)
    gots = (plane_got.at[0], plane_got.at[1], plane_got_e)
    fulls = (full.at[0, core], full.at[1, core], full_e)

    def plane_sends(job):
        me = plane_index(job)
        send_plane(job, lambda n: parts[job].at[n], gots[job].at[me], sems(job, PLANE))
        gots[job][me] = parts[job][me]

    def start_plane(job):
        wait_one(pair_got.at[job], job_recv.at[job, PAIR])
        total = (own[job, core].astype(F32) + pair_got[job].astype(F32)).astype(BF16)
        for n in range(16):
            part[job, n] = total[16 * (n // 2) : 16 * (n // 2) + 16, 256 * (n % 2) : 256 * (n % 2) + 256]
        plane_sends(job)

    def start_plane_e(gradient):
        total = gradient.astype(BF16)
        for n in range(32):
            part_e[n] = total[16 * (n // 2) : 16 * (n // 2) + 16, 256 * (n % 2) : 256 * (n % 2) + 256]
        plane_sends(2)

    def start_line(job):
        wait_all(gots[job], job_recv.at[job, PLANE])
        me = where_am_i()[LINES[job]]
        line_got[job, me] = sum_blocks(gots[job], gots[job].shape[0]).astype(BF16)
        send_line(LINES[job], line_got.at[job, me], sems(job, LINE))

    def start_plane_all(job):
        wait_all(line_got.at[job], job_recv.at[job, LINE])
        block = fulls[job].at[plane_index(job)]
        block[...] = sum_blocks(line_got.at[job], 4).astype(BF16)
        send_plane(job, lambda n: block, block, sems(job, PLANE_ALL))

    def start_mate(job):
        wait_all(fulls[job], job_recv.at[job, PLANE_ALL])
        send_mate(fulls[job], fulls[job], sems(job, MATE))

    for t in range(4, 8):
        second_layer_back(t, back, slope2, second)
    for half in range(2):
        part_of = pl.ds(256 * half, 256)
        start_pair(half, mixer_early[part_of, :] + product(act_t, part_of, late, second))
    for t in range(TILES):
        first_layer_back(t, second, mixer_t, slope1, first)
    start_plane(0)
    start_plane(1)
    start_plane_e(jnp.dot(rows_t[...], first[...], preferred_element_type=F32))

    wait_one(head_pair, head_recv.at[0])
    head_line(1, head_grad[...] + head_pair[...])
    for copy in halos:
        copy.wait()
    place_halos(x_halo, y_halo, field, y_edge)
    start_line(0)
    start_line(1)
    head_line(2, head_line_sum(1))
    send_all("by", lambda peer: slot_part, slot_got.at[by], slot_sems.at[0], slot_sems.at[1])
    slot_got[by] = slot_part[...]
    diffuse(0, field, y_edge, moved)
    start_plane_all(0)
    start_plane_all(1)
    start_line(2)
    head_line(0, head_line_sum(2))
    diffuse(1, field, y_edge, moved)
    start_plane_all(2)
    wait_all(slot_got, slot_sems.at[1])
    slots[...] = read_slots(slot_got)
    diffuse(2, field, y_edge, moved)
    start_mate(0)
    start_mate(1)
    diffuse(3, field, y_edge, moved)
    head_total[...] = head_line_sum(0)
    wait_all(full_e, job_recv.at[2, PLANE_ALL])
    for job in range(2):
        wait_one(full.at[job, 1 - core], job_recv.at[job, MATE])
    wait_all(slot_got, slot_sems.at[0])
    wait_one(head_pair, head_send.at[0])
    for axis in range(3):
        wait_all(head_got.at[axis], head_send.at[axis + 1])
    for job in range(3):
        wait_all(gots[job], job_send.at[job, PLANE])
        wait_all(line_got.at[job], job_send.at[job, LINE])
        wait_all(fulls[job], job_send.at[job, PLANE_ALL])
    for job in range(2):
        wait_one(pair_got.at[job], job_send.at[job, PAIR])
        wait_one(fulls[job], job_send.at[job, MATE])


def scale_of(square_sum, count):
    return lax.rsqrt(jnp.sum(square_sum, keepdims=True) * (1.0 / count) + EPSILON)


def write_sum(blocks, wide, out, sems):
    total = jnp.zeros((16, 256), F32)
    for block in blocks:
        value = block[...].astype(F32)
        total = total + value * value
    scale = scale_of(total, len(blocks) * 16 * 256)
    copies = []
    for n, block in enumerate(blocks):
        wide[pl.ds(16 * (n // 2), 16), pl.ds(256 * (n % 2), 256)] = block[...].astype(F32) * scale
        if n % 16 == 15:
            rows = pl.ds(128 * (n // 16), 128)
            copies.append(pltpu.make_async_copy(wide.at[rows], out.at[rows], sems.at[n // 16]))
            copies[-1].start()
    return copies


def finish_kernel(
    moved, full, full_e, head_total, slots, flow_out, slot_out, embed_out, mixer_out, head_out,
    slot_wide, head_wide, embed_wide, mixer_wide, flow_sems, small_sems, embed_sems, mixer_sems,
):
    copies = []
    for n in range(8):
        part = pl.ds(COLS // 8 * n, COLS // 8)
        copies.append(pltpu.make_async_copy(moved.at[part], flow_out.at[part], flow_sems.at[n]))
    for copy in copies:
        copy.start()
    total = head_total[...]
    total = total * scale_of(total * total, 3 * HID)
    for k in range(3):
        head_wide[k : k + 1, 0:256] = total[k : k + 1]
        head_wide[k : k + 1, 256:512] = total[k + 3 : k + 4]
        slot_wide[k] = slots[k : k + 1, 0:64]
    for n, (source, target) in enumerate(((slot_wide, slot_out), (head_wide, head_out))):
        copies.append(pltpu.make_async_copy(source, target, small_sems.at[n]))
        copies[-1].start()
    copies += write_sum(
        [full.at[j, h, n] for j in range(2) for h in range(2) for n in range(16)],
        mixer_wide, mixer_out, mixer_sems,
    )
    copies += write_sum([full_e.at[n] for n in range(32)], embed_wide, embed_out, embed_sems)
    for copy in copies:
        copy.wait()


SCRATCH = [
    pltpu.SMEM((3, 1, PB), jnp.int32),
    pltpu.VMEM((1, PB), jnp.int32),
    pltpu.VMEM((3, PB), BF16),
    pltpu.VMEM((3, HID), F32),
    pltpu.VMEM((2, CHAN * SLAB, 128), F32),
    pltpu.VMEM((CY * CZ + 32, 128), F32),
    pltpu.VMEM((512, 1024), BF16),
    pltpu.VMEM((1024, 1024), BF16),
    pltpu.VMEM((2048, FEAT), BF16),
    pltpu.VMEM((FEAT, HID), F32),
    pltpu.VMEM((HID, HID), F32),
    pltpu.VMEM((FEAT, HID), BF16),
    pltpu.VMEM((HID, HID), BF16),
    pltpu.VMEM((HID, HID), BF16),
    pltpu.VMEM((2048, HID), BF16),
    pltpu.VMEM((2048, HID), F32),
    pltpu.VMEM((2048, HID), F32),
    pltpu.VMEM((TILES, 4, HID), F32),
    pltpu.VMEM((TILES, 4, HID), F32),
    pltpu.VMEM((2048, HID), BF16),
    pltpu.VMEM((2048, HID), BF16),
    pltpu.VMEM((FEAT, 2048), BF16),
    pltpu.VMEM((HID, 2048), BF16),
    pltpu.VMEM((HID, HID), F32),
    pltpu.VMEM((2, 2, CHAN * CY, 128), BF16),
    pltpu.VMEM((2, 2, CHAN * CX, 128), BF16),
    pltpu.VMEM((2, 2, CHAN * CY, 128), BF16),
    pltpu.VMEM((2, 2, CHAN * CX, 128), BF16),
    pltpu.VMEM((2, 2, CHAN * CX, 128), F32),
    pltpu.VMEM((8, 256), F32),
    pltpu.VMEM((8, 256), F32),
    pltpu.VMEM((3, 4, 8, 256), F32),
    pltpu.VMEM((8, 128), F32),
    pltpu.VMEM((BY, 8, 128), F32),
    pltpu.VMEM((2, 2, 128, HID), BF16),
    pltpu.VMEM((2, 128, HID), BF16),
    pltpu.VMEM((2, 16, 16, 256), BF16),
    pltpu.VMEM((2, 16, 16, 256), BF16),
    pltpu.VMEM((3, 4, 16, 256), BF16),
    pltpu.VMEM((32, 16, 256), BF16),
    pltpu.VMEM((32, 16, 256), BF16),
    pltpu.SemaphoreType.DMA((3, 2, CHAN)),
    pltpu.SemaphoreType.DMA((6,)),
    pltpu.SemaphoreType.DMA((4,)),
    pltpu.SemaphoreType.DMA((4,)),
    pltpu.SemaphoreType.DMA((2,)),
    pltpu.SemaphoreType.DMA((4,)),
    pltpu.SemaphoreType.DMA((4,)),
    pltpu.SemaphoreType.DMA((3, 5)),
    pltpu.SemaphoreType.DMA((3, 5)),
]


def per_device(
    flow_field, patch_corners, patch_learner, drag_target, embed_weight, mixer_weight, head_weight
):
    vmem = pl.BlockSpec(memory_space=pltpu.VMEM)
    anywhere = pl.BlockSpec(memory_space=pl.ANY)
    parts = pl.pallas_call(
        step_kernel,
        out_shape=(
            pltpu.VMEM((COLS, CZ), F32),
            pltpu.VMEM((2, 2, 16, 16, 256), BF16),
            pltpu.VMEM((32, 16, 256), BF16),
            pltpu.VMEM((8, 256), F32),
            pltpu.VMEM((8, 128), F32),
        ),
        in_specs=[anywhere] * 7,
        out_specs=(vmem,) * 5,
        scratch_shapes=SCRATCH,
        compiler_params=pltpu.CompilerParams(
            collective_id=0, has_side_effects=True, vmem_limit_bytes=44 * 2**20
        ),
    )(
        *(
            pltpu.with_memory_space_constraint(value, pltpu.HBM)
            for value in (
                patch_corners, flow_field.reshape(CHAN * CX, CY, CZ), patch_learner.reshape(1, PB),
                drag_target.reshape(3, PB), embed_weight, mixer_weight, head_weight,
            )
        )
    )
    flow, slots, embed, mixer, head = pl.pallas_call(
        finish_kernel,
        out_shape=(
            jax.ShapeDtypeStruct((COLS, CZ), F32),
            jax.ShapeDtypeStruct((3, 1, 64), F32),
            jax.ShapeDtypeStruct((FEAT, HID), F32),
            jax.ShapeDtypeStruct((HID, HID), F32),
            jax.ShapeDtypeStruct((3, HID), F32),
        ),
        in_specs=[vmem] * 5,
        out_specs=(anywhere,) * 5,
        scratch_shapes=[
            pltpu.VMEM((3, 1, 64), F32),
            pltpu.VMEM((3, HID), F32),
            pltpu.VMEM((FEAT, HID), F32),
            pltpu.VMEM((HID, HID), F32),
            pltpu.SemaphoreType.DMA((8,)),
            pltpu.SemaphoreType.DMA((2,)),
            pltpu.SemaphoreType.DMA((2,)),
            pltpu.SemaphoreType.DMA((4,)),
        ],
        compiler_params=pltpu.CompilerParams(vmem_limit_bytes=16 * 2**20),
    )(*parts)
    return flow.reshape(CHAN, CX, CY, CZ), slots, embed, mixer, head


def solution(mesh):
    return jax.shard_map(
        per_device,
        mesh=mesh,
        in_specs=(
            P(None, "bx", "by", None),
            P(None, "bx", "by"),
            P("bx", "by", None),
            P(None, "bx", "by"),
            P(),
            P(),
            P(),
        ),
        out_specs=(P(None, "bx", "by", None), P(None, "bx", "by"), P(), P(), P()),
        check_vma=False,
    )
```
